32 devices in a mesh: case: 2 (over x), elem: 16 (over z, y, core).
Axes of the slice: x: 2, y: 2, z: 4, core: 2. Of those that a mesh axis runs over, the one named last changes fastest.
Arguments:
- records: bfloat16 [32768, 128], P(('case', 'elem')), parts along dimension 0, may hold values from -6 to 6
- panel_owner: int32 [16384, 1], P('elem'), may hold values from 0 to 15; in each aligned block of 1024 rows (0 to 1023, 1024 to 2047, ...) at most 128 rows name the same one
- panel_slot: int32 [16384], P('elem'), may hold values from 0 to 3071
- stiff_blocks: bfloat16 [512, 3, 96, 96], P('elem'), may hold values from -0.375 to 0.375
- block_cols: int32 [512, 3], P('elem'), may hold values from 0 to 511, as said below
- modes: bfloat16 [49152, 1024], P('elem'), may hold values from -0.02734375 to 0.02734375
- admittance: float32 [2048, 1024], P('case'), parts along dimension 0, may hold values from -3 to 3
Outputs:
- adjoint: bfloat16 [98304, 128], P(('case', 'elem')), parts along dimension 0
- sensitivity: float32 [98304], P(('case', 'elem')), parts along dimension 0
The draws below stay inside these ranges and needn't reach their ends.
There are 2 independent parts, one for each index of `case`. The reference program is written for one: setup_inputs(seed, part) draws one part's arguments, and reference() takes and returns one part's arrays. A program takes and returns all parts, laid end to end along the dimension named above; an argument that names none is the same for every part. Nothing has to cross between parts.
Inputs may be any that keep to these rules, and one draw needn't show every extreme that they name: `panel_owner`: among the 1024 panels of one device no owner appears more than 128 times, and in some device's panels some owner appears exactly 128 times. `block_cols`: each stored block's column block lies within 8 blocks of its row block; column 0 lies exactly 8 blocks away unless the grid's end clips it.
All inputs are finite; a program needn't handle non-finite values.
Results may differ from the reference program's by a relative error of at most 0.0062.
Values may be sent and summed in bfloat16 or wider, within the bound.
No kernel may reach another device: no remote copies, remote signals or barrier semaphores. Data moves between devices by JAX's collectives and lax.ppermute only.
A program may use at most 64 MiB of HBM per device.

```python
import math
import jax
import jax.numpy as jnp
import numpy as np
from jax import lax

R = 128
M = 1024
BS = 96
NNZ = 3
REACH = 8
PAN_DEV = 1024
BLK_DEV = 32
CAP = 128
E_DEV = 3072
PANELS = 16384
ELEMS = 49152
NBLK = 512
N_ELEM = 16


def draw_block_cols(key, part):
    row_blocks = jnp.arange(NBLK, dtype=jnp.int32)
    key_one, key_two, key_three = jax.random.split(jax.random.fold_in(key, 11), 3)
    direction = jax.random.randint(key_one, (NBLK,), 0, 2).astype(jnp.int32) * 2 - 1
    far_cols = jnp.clip(row_blocks + direction * REACH, 0, NBLK - 1)
    near_one = jnp.clip(row_blocks + jax.random.randint(key_two, (NBLK,), -REACH, REACH + 1).astype(jnp.int32), 0, NBLK - 1)
    near_two = jnp.clip(row_blocks + jax.random.randint(key_three, (NBLK,), -REACH, REACH + 1).astype(jnp.int32), 0, NBLK - 1)
    return jnp.stack([far_cols, near_one, near_two], axis=1).astype(jnp.int32)


def touch_ends(result, rng, smallest, high):
    longest = result.shape.index(max(result.shape))
    spots = []
    for shift in (0, 1):
        where = [jax.random.randint(jax.random.fold_in(rng, axis), (), 0, length) for axis, length in enumerate(result.shape)]
        where[longest] = (where[longest] + shift) % result.shape[longest]
        spots.append(tuple(where))
    return result.at[spots[0]].set(smallest).at[spots[1]].set(high)


def shard_levels(rng, extent, cuts, least, largest):
    level, own = 1.0, jax.random.fold_in(rng, 6)
    for axis_at, shards_of in cuts:
        draws = jnp.exp(jax.random.uniform(jax.random.fold_in(own, axis_at), (shards_of,), jnp.float32, least / len(cuts), largest / len(cuts)))
        level = level * jnp.repeat(draws, extent[axis_at] // shards_of).reshape([-1 if axis == axis_at else 1 for axis in range(len(extent))])
    return level


def assign_block(key, own, number, rows, number_of, top, bound, skew):
    ranking = jax.random.permutation(key, number_of)
    crowded, common = load_shares(number_of, rows * top, bound, skew, True), load_shares(number_of, rows * top, bound, skew, False)
    places = jnp.arange(number_of)

    def named(tallies, turn):
        used = int((tallies > 0).sum())
        fixed = max(1, used // 4)
        moved = fixed + (places - fixed + turn * (used - fixed)) % max(1, number_of - fixed)
        return jnp.zeros((number_of,), jnp.int32).at[ranking[jnp.where(places < fixed, places, moved)]].set(jnp.asarray(tallies, jnp.int32))

    tallies = jnp.where(number % 4 == 0, named(crowded, number // 4), named(common, number - number // 4 - 1))
    mixed = jax.random.permutation(jax.random.fold_in(own, 3), number_of)
    giver, taker = mixed[0:number_of // 2 * 2:2], mixed[1:number_of // 2 * 2:2]
    slack = jnp.minimum(tallies[giver] - 1, bound - tallies[taker]) // 2
    slack = jnp.where((giver == ranking[0]) | (taker == ranking[0]) | (tallies[taker] == 0), 0, jnp.maximum(slack, 0))
    moved = jax.random.randint(jax.random.fold_in(own, 4), (number_of // 2,), 0, 1 << 20) % (slack + 1)
    tallies = tallies.at[giver].add(-moved).at[taker].add(moved)
    items = jnp.searchsorted(jnp.cumsum(tallies), jnp.arange(rows * top), side="right").astype(jnp.int32)
    grid = items.reshape(top, rows).T
    grid = grid[jax.random.permutation(jax.random.fold_in(own, 1), rows)]
    turn = jax.random.randint(jax.random.fold_in(own, 2), (rows, 1), 0, top)
    return jnp.take_along_axis(grid, (jnp.arange(top)[None, :] + turn) % top, axis=1)


def load_shares(number_of, total, bound, skew, full):
    portions = [(1 << 20) // math.isqrt(standing ** skew) + 1 for standing in range(1, number_of + 1)]
    largest = bound if full else min(bound, max(-(-total // number_of), total * portions[0] // sum(portions)))
    least = 1 if total - largest >= number_of - 1 else 0
    counts, rest = [largest] + [least] * (number_of - 1), total - largest - least * (number_of - 1)
    while rest > 0:
        movable = [i for i in range(1, number_of) if counts[i] < largest] or [i for i in range(1, number_of) if counts[i] < bound]
        whole, remaining = sum([portions[i] for i in movable]), rest
        for i in movable:
            more = min(bound - counts[i], max(1, remaining * portions[i] // whole), rest)
            counts[i] = counts[i] + more
            rest = rest - more
    return np.array(counts)


def normal_values(rng, extent, width, most, cuts=(), kind=jnp.bfloat16):
    drawn = width * jax.random.normal(rng, extent, jnp.float32)
    if cuts:
        drawn = drawn * shard_levels(rng, extent, cuts, -0.22, 0.18)
    return jnp.clip(drawn, -most, most).astype(kind)


def setup_inputs(seed: int = 0, part: int = 0) -> dict:
    arg_keys = jax.random.split(jax.random.key(seed), 8)
    own_keys = jax.random.split(jax.random.fold_in(arg_keys[7], part), 8)
    records = normal_values(own_keys[0], (PANELS, R), 1.0, 6.0, ((0, 16),))
    panel_owner_keys = jax.random.split(jax.random.fold_in(arg_keys[1], 1), PANELS // PAN_DEV)
    panel_owner_turns = jax.random.permutation(jax.random.fold_in(arg_keys[1], 3), PANELS // PAN_DEV)
    panel_owner = jax.vmap(lambda own, number: assign_block(jax.random.fold_in(arg_keys[1], 2), own, number, PAN_DEV, N_ELEM, 1, CAP, 2))(panel_owner_keys, panel_owner_turns).reshape((PANELS, 1))
    panel_slot = touch_ends(jax.random.randint(arg_keys[2], (PANELS,), 0, E_DEV), jax.random.fold_in(arg_keys[2], 1), 0, E_DEV - 1).astype(jnp.int32)
    stiff_blocks = normal_values(arg_keys[3], (NBLK, NNZ, BS, BS), (NNZ * BS) ** -0.5, 0.375, ((0, 16),))
    block_cols = draw_block_cols(jax.random.fold_in(arg_keys[7], 71), part)
    modes = normal_values(arg_keys[5], (ELEMS, M), ELEMS ** -0.5, 0.02734375, ((0, 16),))
    admittance = normal_values(own_keys[6], (M, M), (ELEMS ** 0.5 / M), 3.0, (), jnp.float32)
    return dict(records=records, panel_owner=panel_owner, panel_slot=panel_slot, stiff_blocks=stiff_blocks, block_cols=block_cols, modes=modes, admittance=admittance)


def reference(records, panel_owner, panel_slot, stiff_blocks, block_cols, modes, admittance):
    elem_ids = (panel_owner[:, 0] * E_DEV + panel_slot).astype(jnp.int32)
    elem_load = jax.ops.segment_sum(records.astype(jnp.float32), elem_ids, num_segments=ELEMS).astype(jnp.bfloat16)
    blocks = elem_load.reshape(NBLK, BS, R)

    def row_group(group):
        stiff_part, col_part = group
        picked = blocks[col_part]
        return jnp.einsum('bjrs,bjsc->brc', stiff_part.astype(jnp.float32), picked.astype(jnp.float32))

    stiffened = lax.map(row_group, (stiff_blocks.reshape(N_ELEM, BLK_DEV, NNZ, BS, BS), block_cols.reshape(N_ELEM, BLK_DEV, NNZ)))
    stiffened = stiffened.reshape(ELEMS, R).astype(jnp.bfloat16)
    modal = lax.dot_general(modes, stiffened, (((0,), (0,)), ((), ())), preferred_element_type=jnp.float32)
    adj_modes = jnp.dot(admittance, modal, precision=lax.Precision.HIGHEST).astype(jnp.bfloat16)
    adjoint = jnp.dot(modes, adj_modes, preferred_element_type=jnp.float32)
    sensitivity = jnp.sum(adjoint * stiffened.astype(jnp.float32), axis=1)
    return adjoint.astype(jnp.bfloat16), sensitivity
```

```python
import functools

import jax
import jax.numpy as jnp
from jax import lax
from jax.experimental import pallas as pl
from jax.experimental.pallas import tpu as pltpu
from jax.sharding import PartitionSpec as P

LANES = 128
TAIL = 16
REACH = 8
BF = jnp.bfloat16
F32 = jnp.float32
NT = (((1,), (1,)), ((), ()))
TN = (((0,), (0,)), ((), ()))


def call(kernel, out_shape, *operands, smem=(), scratch=(), flops=0, limit=48 * 2**20):
    space = [pltpu.SMEM if k in smem else pltpu.VMEM for k in range(len(operands))]
    moved = sum(x.size * x.dtype.itemsize for x in operands)
    return pl.pallas_call(
        kernel,
        out_shape=out_shape,
        in_specs=[pl.BlockSpec(memory_space=s) for s in space],
        out_specs=jax.tree.map(lambda _: pl.BlockSpec(memory_space=pltpu.VMEM), out_shape),
        scratch_shapes=list(scratch),
        compiler_params=pltpu.CompilerParams(vmem_limit_bytes=limit),
        cost_estimate=pl.CostEstimate(flops=flops, bytes_accessed=moved, transcendentals=0),
    )(*operands)


def shape(dims, dtype):
    return jax.ShapeDtypeStruct(dims, dtype)


def hot(rows, key):
    row = lax.broadcasted_iota(jnp.int32, (rows, key.shape[1]), 0).astype(F32).astype(BF)
    return jnp.where(row == key, jnp.ones((), BF), jnp.zeros((), BF))


def pack_kernel(owners, cap, owner_ref, slot_ref, rec_ref, out_ref):
    pan = rec_ref.shape[0]
    pieces = pan // LANES
    owner = owner_ref[...]
    match = lax.broadcasted_iota(jnp.int32, (owners, pan), 0) == owner
    match_f = jnp.where(match, 1.0, 0.0)
    before = lax.broadcasted_iota(jnp.int32, (LANES, LANES), 0)
    after = lax.broadcasted_iota(jnp.int32, (LANES, LANES), 1)
    triangle = jnp.where(before <= after, 1.0, 0.0).astype(BF)
    stacked = jnp.concatenate(
        [match_f[:, k * LANES : (k + 1) * LANES] for k in range(pieces)], axis=0
    ).astype(BF)
    running = jnp.dot(stacked, triangle, preferred_element_type=F32)
    offset = jnp.zeros((owners, 1), F32)
    ranks = []
    for k in range(pieces):
        piece = running[k * owners : (k + 1) * owners] + offset
        picked = match_f[:, k * LANES : (k + 1) * LANES] * piece
        ranks.append(jnp.sum(picked, axis=0, keepdims=True) - 1.0)
        offset = piece[:, LANES - 1 : LANES]
    rank = jnp.concatenate(ranks, axis=1)
    slot = jnp.concatenate([slot_ref[k : k + 1, :] for k in range(pieces)], axis=1)
    high = (slot >> 6).astype(F32)
    low = (slot & 63).astype(F32)
    weights = jnp.concatenate([match_f * high, match_f * low], axis=0).astype(BF)
    share = LANES // cap
    shift = lax.rem(lax.axis_index("elem"), share) * cap
    spread = hot(LANES, (rank + shift.astype(F32)).astype(BF))
    slots = lax.dot_general(weights, spread, NT, preferred_element_type=F32)
    records = rec_ref[...]
    tail_row = lax.broadcasted_iota(jnp.int32, (TAIL, LANES), 0)
    for o in range(owners):
        key = jnp.where(owner == o, rank, -1.0).astype(BF)
        out_ref[o, 0:cap, :] = jnp.dot(
            hot(cap, key), records, preferred_element_type=F32
        ).astype(BF)
        tail = jnp.where(
            tail_row == 0,
            slots[o : o + 1],
            jnp.where(tail_row == 1, slots[owners + o : owners + o + 1], 0.0),
        )
        out_ref[o, cap : cap + TAIL, :] = tail.astype(BF)


def read_slots(got_ref, cap):
    owners = got_ref.shape[0]
    share = LANES // cap
    rows = []
    for group in range(owners // share):
        tail = got_ref[group * share, cap : cap + TAIL, :].astype(F32)
        for k in range(1, share):
            tail += got_ref[group * share + k, cap : cap + TAIL, :].astype(F32)
        rows.append(tail[0:1] * 64.0 + tail[1:2])
    return jnp.concatenate(rows, axis=1)


def loads_at(slots, records, base, rows):
    key = slots - base.astype(F32)
    key = jnp.where((key >= 0.0) & (key < float(rows)), key, -1.0).astype(BF)
    return jnp.dot(hot(rows, key), records, preferred_element_type=F32).astype(BF)


def edge_kernel(cap, elem_rows, halo, got_ref, near_ref, far_ref):
    odd = lax.rem(lax.axis_index("elem"), 2)
    slots = read_slots(got_ref, cap)
    records = got_ref[:, 0:cap, :].reshape(-1, LANES)
    last = elem_rows - halo
    chunk = 256
    for k in range(halo // chunk):
        base = jnp.where(odd == 1, last, 0) + k * chunk
        far_ref[k * chunk : (k + 1) * chunk, :] = loads_at(slots, records, base, chunk)
    for k in range(halo // chunk):
        base = jnp.where(odd == 1, 0, last) + k * chunk
        near_ref[k * chunk : (k + 1) * chunk, :] = loads_at(slots, records, base, chunk)


def stiffen(stiff_ref, cols_ref, ext_ref, block, first_col):
    size = stiff_ref.shape[2]
    total = None
    for j in range(stiff_ref.shape[1]):
        start = pl.multiple_of((cols_ref[j, block] - first_col) * size, 32)
        part = jnp.dot(
            stiff_ref[block, j], ext_ref[pl.ds(start, size), :], preferred_element_type=F32
        )
        total = part if total is None else total + part
    return total.astype(BF)


def middle_kernel(
    cap, halo, got_ref, near_ref, far_ref, stiff_ref, cols_ref, modes_ref,
    loads_ref, st_ref, modal_ref,
):
    elem_rows = modes_ref.shape[0]
    blocks, _, size, _ = stiff_ref.shape
    me = lax.axis_index("elem")
    odd = lax.rem(me, 2)
    last = elem_rows - halo
    near_at = pl.multiple_of(jnp.where(odd == 1, 0, last), 32)
    far_at = pl.multiple_of(jnp.where(odd == 1, last, 0), 32)
    loads_ref[pl.ds(near_at, halo), :] = near_ref[...]
    loads_ref[pl.ds(far_at, halo), :] = far_ref[...]
    slots = read_slots(got_ref, cap)
    records = got_ref[:, 0:cap, :].reshape(-1, LANES)
    chunk = 256
    for k in range((last - halo) // chunk):
        base = halo + k * chunk
        loads_ref[base : base + chunk, :] = loads_at(slots, records, jnp.int32(base), chunk)
    for b in range(REACH, blocks - REACH):
        st_ref[(b - REACH) * size : (b - REACH + 1) * size, :] = stiffen(
            stiff_ref, cols_ref, loads_ref, b, me * blocks
        )
    modal_ref[...] = lax.dot_general(
        st_ref[...], modes_ref[halo:last, :], TN, preferred_element_type=F32
    )


def outer_kernel(
    halo, loads_ref, near_ref, far_ref, stiff_ref, cols_ref, modes_ref, modal_ref,
    st_ref, keep_ref, send_ref, ext_ref, total_ref,
):
    elem_rows = modes_ref.shape[0]
    blocks, _, size, _ = stiff_ref.shape
    me = lax.axis_index("elem")
    odd = lax.rem(me, 2)
    last = elem_rows - halo
    end = halo + elem_rows
    near_at = pl.multiple_of(jnp.where(odd == 1, 0, end), 32)
    far_at = pl.multiple_of(jnp.where(odd == 1, end, 0), 32)
    ext_ref[pl.ds(near_at, halo), :] = near_ref[...]
    ext_ref[pl.ds(far_at, halo), :] = far_ref[...]
    ext_ref[halo:end, :] = loads_ref[...]
    first_col = me * blocks - REACH
    for k in range(REACH):
        st_ref[k * size : (k + 1) * size, :] = stiffen(
            stiff_ref, cols_ref, ext_ref, k, first_col
        )
        st_ref[halo + k * size : halo + (k + 1) * size, :] = stiffen(
            stiff_ref, cols_ref, ext_ref, blocks - REACH + k, first_col
        )
    total_ref[...] = (
        modal_ref[...]
        + lax.dot_general(st_ref[0:halo, :], modes_ref[0:halo, :], TN, preferred_element_type=F32)
        + lax.dot_general(st_ref[halo:, :], modes_ref[last:, :], TN, preferred_element_type=F32)
    )
    half = total_ref.shape[0] // 2
    keep_ref[...] = total_ref[pl.ds(pl.multiple_of(odd * half, 8), half), :]
    send_ref[...] = total_ref[pl.ds(pl.multiple_of((1 - odd) * half, 8), half), :]


def pair_kernel(mine_ref, other_ref, keep_ref, send_ref, total_ref):
    bit = lax.rem(lax.axis_index("elem") // 2, 2)
    total_ref[...] = mine_ref[...] + other_ref[...]
    half = total_ref.shape[0] // 2
    keep_ref[...] = total_ref[pl.ds(pl.multiple_of(bit * half, 8), half), :]
    send_ref[...] = total_ref[pl.ds(pl.multiple_of((1 - bit) * half, 8), half), :].astype(BF)


def add_kernel(mine_ref, other_ref, total_ref, send_ref):
    total = mine_ref[...] + other_ref[...].astype(F32)
    total_ref[...] = total
    send_ref[...] = total.astype(BF)


def split_kernel(a_ref, high_ref, low_ref):
    a = a_ref[...]
    high = a.astype(BF)
    high_ref[...] = high
    low_ref[...] = (a - high.astype(F32)).astype(BF)


def admit_kernel(count, mine_ref, *refs):
    others, (high_ref, low_ref, adj_ref) = refs[:count], refs[count:]
    total = mine_ref[...]
    for other in others:
        total += other[...].astype(F32)
    high = total.astype(BF)
    low = (total - high.astype(F32)).astype(BF)
    adj = lax.dot_general(high, high_ref[...], NT, preferred_element_type=F32)
    adj += lax.dot_general(high, low_ref[...], NT, preferred_element_type=F32)
    adj += lax.dot_general(low, high_ref[...], NT, preferred_element_type=F32)
    adj_ref[...] = adj.astype(BF)


def back_kernel(halo, own_ref, y_ref, core_ref, both_ref, modes_ref, mid_ref, out_ref, adj_ref, sens_ref, field_ref):
    me = lax.axis_index("elem")
    odd = lax.rem(me, 2)
    bit = lax.rem(me // 2, 2)
    quarter = own_ref.shape[0]
    for ref, c, y in (
        (own_ref, odd, bit),
        (y_ref, odd, 1 - bit),
        (core_ref, 1 - odd, bit),
        (both_ref, 1 - odd, 1 - bit),
    ):
        at = pl.multiple_of((2 * c + y) * quarter, 16)
        field_ref[pl.ds(at, quarter), :] = ref[...]
    field = field_ref[...]
    elem_rows = modes_ref.shape[0]
    last = elem_rows - halo
    chunk = 256
    for k in range(elem_rows // chunk):
        at = k * chunk
        part = lax.dot_general(
            modes_ref[at : at + chunk, :], field, NT, preferred_element_type=F32
        )
        adj_ref[at : at + chunk, :] = part.astype(BF)
        if at < halo:
            st = out_ref[at : at + chunk, :]
        elif at < last:
            st = mid_ref[at - halo : at - halo + chunk, :]
        else:
            st = out_ref[at - last + halo : at - last + halo + chunk, :]
        product = part * st.astype(F32)
        for i in range(chunk // LANES):
            row = jnp.sum(product[i * LANES : (i + 1) * LANES, :].T, axis=0, keepdims=True)
            sens_ref[at // LANES + i : at // LANES + i + 1, :] = row


def body(records, panel_owner, panel_slot, stiff_blocks, block_cols, modes, admittance):
    owners = lax.axis_size("elem")
    pan, width = records.shape
    cap = 2 * pan // owners
    elem_rows, mode_count = modes.shape
    blocks, nnz, size, _ = stiff_blocks.shape
    halo = REACH * size

    def swap(array, mask):
        return lax.ppermute(array, "elem", [(i, i ^ mask) for i in range(owners)])

    def swap_far(array):
        pairs = [(i, i + 1) for i in range(1, owners - 1, 2)]
        return lax.ppermute(array, "elem", pairs + [(j, i) for i, j in pairs])

    packed = call(
        functools.partial(pack_kernel, owners, cap),
        shape((owners, cap + TAIL, width), BF),
        panel_owner.reshape(1, pan),
        panel_slot.reshape(pan // LANES, LANES),
        records,
        flops=2 * owners * cap * pan * width,
    )
    got = lax.all_to_all(packed, "elem", split_axis=0, concat_axis=0, tiled=True)
    a_high, a_low = call(
        split_kernel,
        (shape(admittance.shape, BF), shape(admittance.shape, BF)),
        admittance,
        flops=4 * admittance.size,
    )
    near, far = call(
        functools.partial(edge_kernel, cap, elem_rows, halo),
        (shape((halo, width), BF), shape((halo, width), BF)),
        got,
        flops=2 * owners * cap * 2 * halo * width,
    )
    got_far = swap_far(far)
    got_near = swap(near, 1)
    cols = block_cols.T
    loads, st_mid, modal_mid = call(
        functools.partial(middle_kernel, cap, halo),
        (
            shape((elem_rows, width), BF),
            shape((elem_rows - 2 * halo, width), BF),
            shape((width, mode_count), F32),
        ),
        got, near, far, stiff_blocks, cols, modes,
        smem=(4,),
        flops=elem_rows * width * mode_count,
    )
    st_out, keep, send = call(
        functools.partial(outer_kernel, halo),
        (
            shape((2 * halo, width), BF),
            shape((width // 2, mode_count), F32),
            shape((width // 2, mode_count), F32),
        ),
        loads, got_near, got_far, stiff_blocks, cols, modes, modal_mid,
        smem=(4,),
        scratch=(pltpu.VMEM((elem_rows + 2 * halo, width), BF), pltpu.VMEM((width, mode_count), F32)),
        flops=elem_rows * width * mode_count,
    )
    quarter = width // 4
    keep, send = call(
        pair_kernel,
        (shape((quarter, mode_count), F32), shape((quarter, mode_count), BF)),
        keep, swap(send, 1),
        scratch=(pltpu.VMEM((width // 2, mode_count), F32),),
    )
    total, send = call(
        add_kernel,
        (shape((quarter, mode_count), F32), shape((quarter, mode_count), BF)),
        keep, swap(send, 2),
    )
    groups = owners // 4
    others = [swap(send, 4 * k) for k in reversed(range(1, groups))]
    own = call(
        functools.partial(admit_kernel, len(others)),
        shape((quarter, mode_count), BF),
        total, *others, a_high, a_low,
        flops=6 * quarter * mode_count * mode_count,
    )
    across = swap(own, 2)
    beside = swap(own, 1)
    both = swap(across, 1)
    adjoint, sensitivity = call(
        functools.partial(back_kernel, halo),
        (shape((elem_rows, width), BF), shape((elem_rows // LANES, LANES), F32)),
        own, across, beside, both, modes, st_mid, st_out,
        scratch=(pltpu.VMEM((width, mode_count), BF),),
        flops=2 * elem_rows * width * mode_count,
    )
    return adjoint, sensitivity.reshape(elem_rows)


def solution(mesh):
    in_specs = (
        P(("case", "elem"), None),
        P("elem", None),
        P("elem"),
        P("elem", None, None, None),
        P("elem", None),
        P("elem", None),
        P("case", None),
    )
    out_specs = (P(("case", "elem"), None), P(("case", "elem")))
    return jax.shard_map(body, mesh=mesh, in_specs=in_specs, out_specs=out_specs, check_vma=False)
```

```python
import functools

import jax
import jax.numpy as jnp
from jax import lax
from jax.experimental import pallas as pl
from jax.experimental.pallas import tpu as pltpu
from jax.sharding import PartitionSpec as P

LANES = 128
TAIL = 16
REACH = 8
BF = jnp.bfloat16
F32 = jnp.float32
NT = (((1,), (1,)), ((), ()))
NN = (((1,), (0,)), ((), ()))
TN = (((0,), (0,)), ((), ()))


def call(kernel, out_shape, *operands, smem=(), hbm=(), out=pltpu.VMEM, scratch=(), flops=0, limit=16 * 2**20):
    space = [
        pltpu.SMEM if k in smem else pltpu.HBM if k in hbm else pltpu.VMEM
        for k in range(len(operands))
    ]
    moved = sum(x.size * x.dtype.itemsize for x in operands)
    return pl.pallas_call(
        kernel,
        out_shape=out_shape,
        in_specs=[pl.BlockSpec(memory_space=s) for s in space],
        out_specs=jax.tree.map(lambda _: pl.BlockSpec(memory_space=out), out_shape),
        scratch_shapes=list(scratch),
        compiler_params=pltpu.CompilerParams(vmem_limit_bytes=limit),
        cost_estimate=pl.CostEstimate(flops=flops, bytes_accessed=moved, transcendentals=0),
    )(*operands)


def shape(dims, dtype):
    return jax.ShapeDtypeStruct(dims, dtype)


def odd_core():
    return lax.rem(lax.axis_index("elem"), 2)


def hot(rows, key):
    row = lax.broadcasted_iota(jnp.int32, (rows, key.shape[1]), 0).astype(F32).astype(BF)
    return jnp.where(row == key, jnp.ones((), BF), jnp.zeros((), BF))


def write_messages(cross, cap, chips, owner, rank, records, slots_ref, out_ref):
    me = lax.axis_index("elem")
    core = lax.rem(me + cross, 2)
    y, z = lax.rem(me // 2, 2), me // 4
    share, owners = LANES // cap, 2 * chips
    tail_row = lax.broadcasted_iota(jnp.int32, (TAIL, LANES), 0) - 2 * cross
    for j in range(chips):
        dz, dy = j // 2, j % 2
        to = (lax.rem(z + dz, chips // 2) * 2 + lax.rem(y + dy, 2)) * 2 + core
        key = jnp.where(owner == to, rank, -1.0).astype(BF)
        out_ref[j, 0:cap, :] = jnp.dot(
            hot(cap, key), records, preferred_element_type=F32
        ).astype(BF)
        place = (dy * 2 + cross) % share
        high = slots_ref[place, pl.ds(to, 1), :]
        low = slots_ref[place, pl.ds(owners + to, 1), :]
        tail = jnp.where(tail_row == 0, high, jnp.where(tail_row == 1, low, 0.0))
        out_ref[j, cap : cap + TAIL, :] = tail.astype(BF)


def pack_kernel(
    cap, owner_ref, slot_ref, rec_ref, cross_ref, rank_ref, slots_ref, held_ref
):
    pan = rec_ref.shape[0]
    owners = slots_ref.shape[1] // 2
    pieces = pan // LANES
    before = lax.broadcasted_iota(jnp.int32, (LANES, LANES), 0)
    after = lax.broadcasted_iota(jnp.int32, (LANES, LANES), 1)
    triangle = jnp.where(before <= after, 1.0, 0.0).astype(BF)
    owner = owner_ref[...]
    slot = jnp.concatenate([slot_ref[k : k + 1, :] for k in range(pieces)], axis=1)
    held_ref[...] = rec_ref[...]
    match = lax.broadcasted_iota(jnp.int32, (owners, pan), 0) == owner
    match_f = jnp.where(match, 1.0, 0.0)
    stacked = jnp.concatenate(
        [match_f[:, k * LANES : (k + 1) * LANES] for k in range(pieces)], axis=0
    ).astype(BF)
    running = jnp.dot(stacked, triangle, preferred_element_type=F32)
    offset = jnp.zeros((owners, 1), F32)
    ranks = []
    for k in range(pieces):
        piece = running[k * owners : (k + 1) * owners] + offset
        picked = match_f[:, k * LANES : (k + 1) * LANES] * piece
        ranks.append(jnp.sum(picked, axis=0, keepdims=True) - 1.0)
        offset = piece[:, LANES - 1 : LANES]
    rank = jnp.concatenate(ranks, axis=1)
    rank_ref[...] = rank
    high = (slot >> 6).astype(F32)
    low = (slot & 63).astype(F32)
    weights = jnp.concatenate([match_f * high, match_f * low], axis=0).astype(BF)
    for place in range(LANES // cap):
        spread = hot(LANES, (rank + float(place * cap)).astype(BF))
        slots_ref[place] = lax.dot_general(weights, spread, NT, preferred_element_type=F32)
    write_messages(1, cap, owners // 2, owner, rank, rec_ref[...], slots_ref, cross_ref)


def pack_own_kernel(cap, owner_ref, rank_ref, slots_ref, rec_ref, own_ref):
    chips = slots_ref.shape[1] // 4
    write_messages(
        0, cap, chips, owner_ref[...], rank_ref[...], rec_ref[...], slots_ref, own_ref
    )


def merge_kernel(cap, own_ref, cross_ref, *out_refs):
    for j, ref in enumerate(out_refs):
        ref[0:cap] = own_ref[j, 0:cap]
        ref[cap : 2 * cap] = cross_ref[j, 0:cap]
        ref[2 * cap :] = own_ref[j, cap:] + cross_ref[j, cap:]


def loads_at(slots, records, base, rows):
    key = slots - base.astype(F32)
    key = jnp.where((key >= 0.0) & (key < float(rows)), key, -1.0).astype(BF)
    return jnp.dot(hot(rows, key), records, preferred_element_type=F32).astype(BF)


CHUNK = 256


def far_kernel(cap, elem_rows, count, *refs):
    got_refs, (far_ref, slots_ref, records_ref) = refs[:count], refs[count:]
    share = LANES // cap
    order = [(ref, x) for ref in got_refs for x in range(2)]
    for k, ref in enumerate(got_refs):
        records_ref[2 * k * cap : 2 * (k + 1) * cap, :] = ref[0 : 2 * cap, :]
    rows = []
    for group in range(len(order) // share):
        row = None
        for ref, x in order[group * share : (group + 1) * share]:
            tail = ref[2 * cap :, :].astype(F32)
            part = tail[2 * x : 2 * x + 1] * 64.0 + tail[2 * x + 1 : 2 * x + 2]
            row = part if row is None else row + part
        rows.append(row)
    slots = jnp.concatenate(rows, axis=1)
    slots_ref[...] = slots
    halo = far_ref.shape[0]
    first = jnp.where(odd_core() == 1, elem_rows - halo, 0)
    records = records_ref[...]
    for k in range(halo // CHUNK):
        far_ref[k * CHUNK : (k + 1) * CHUNK, :] = loads_at(
            slots, records, first + k * CHUNK, CHUNK
        )


def near_kernel(elem_rows, slots_ref, records_ref, near_ref):
    halo = near_ref.shape[0]
    first = jnp.where(odd_core() == 1, 0, elem_rows - halo)
    for k in range(halo // CHUNK):
        near_ref[k * CHUNK : (k + 1) * CHUNK, :] = loads_at(
            slots_ref[...], records_ref[...], first + k * CHUNK, CHUNK
        )


def stiffen(stiff_ref, cols_ref, loads_ref, block, first_col):
    size = stiff_ref.shape[2]
    total = None
    for j in range(stiff_ref.shape[1]):
        start = pl.multiple_of((cols_ref[j, block] - first_col) * size, 32)
        part = jnp.dot(
            stiff_ref[block, j], loads_ref[pl.ds(start, size), :], preferred_element_type=F32
        )
        total = part if total is None else total + part
    return total.astype(BF)


def middle_kernel(
    slots_ref, records_ref, near_ref, far_ref, stiff_ref, cols_ref, loads_ref, st_ref
):
    elem_rows = loads_ref.shape[0]
    halo = near_ref.shape[0]
    blocks, _, size, _ = stiff_ref.shape
    odd = odd_core()
    last = elem_rows - halo
    near_at = pl.multiple_of(jnp.where(odd == 1, 0, last), 32)
    far_at = pl.multiple_of(jnp.where(odd == 1, last, 0), 32)
    loads_ref[pl.ds(near_at, halo), :] = near_ref[...]
    loads_ref[pl.ds(far_at, halo), :] = far_ref[...]
    for k in range((last - halo) // CHUNK):
        base = halo + k * CHUNK
        loads_ref[base : base + CHUNK, :] = loads_at(
            slots_ref[...], records_ref[...], jnp.int32(base), CHUNK
        )
    first_col = lax.axis_index("elem") * blocks
    for b in range(REACH, blocks - REACH):
        st_ref[(b - REACH) * size : (b - REACH + 1) * size, :] = stiffen(
            stiff_ref, cols_ref, loads_ref, b, first_col
        )


def outer_rows(side, loads_ref, got_ref, stiff_ref, cols_ref, st_ref, ext_ref):
    halo = got_ref.shape[0]
    blocks, _, size, _ = stiff_ref.shape
    end = halo + loads_ref.shape[0]
    got_at = pl.multiple_of(side * end, 32)
    ext_ref[halo:end, :] = loads_ref[...]
    ext_ref[pl.ds(got_at, halo), :] = got_ref[...]
    first_col = lax.axis_index("elem") * blocks - REACH
    for k in range(REACH):
        st_ref[k * size : (k + 1) * size, :] = stiffen(
            stiff_ref, cols_ref, ext_ref, side * (blocks - REACH) + k, first_col
        )


def near_rows_kernel(
    loads_ref, got_ref, stiff_ref, cols_ref, modes_ref, mid_ref, st_ref, modal_ref, ext_ref
):
    side = 1 - odd_core()
    outer_rows(side, loads_ref, got_ref, stiff_ref, cols_ref, st_ref, ext_ref)
    halo = got_ref.shape[0]
    last = modes_ref.shape[0] - halo
    at = pl.multiple_of(side * last, 32)
    modal_ref[...] = lax.dot_general(
        mid_ref[...], modes_ref[halo:last, :], TN, preferred_element_type=F32
    ) + lax.dot_general(
        st_ref[...], modes_ref[pl.ds(at, halo), :], TN, preferred_element_type=F32
    )


def far_rows_kernel(
    loads_ref, got_ref, stiff_ref, cols_ref, modes_ref, near_ref, modal_ref,
    edge_ref, keep_ref, send_ref, ext_ref, st_ref, total_ref,
):
    odd = odd_core()
    outer_rows(odd, loads_ref, got_ref, stiff_ref, cols_ref, st_ref, ext_ref)
    halo = got_ref.shape[0]
    last = modes_ref.shape[0] - halo
    at = pl.multiple_of(odd * last, 32)
    total_ref[...] = modal_ref[...] + lax.dot_general(
        st_ref[...], modes_ref[pl.ds(at, halo), :], TN, preferred_element_type=F32
    )
    half = total_ref.shape[0] // 2
    keep_ref[...] = total_ref[pl.ds(pl.multiple_of(odd * half, 8), half), :]
    send_ref[...] = total_ref[pl.ds(pl.multiple_of((1 - odd) * half, 8), half), :]
    edge_ref[pl.ds(pl.multiple_of(odd * halo, 32), halo), :] = st_ref[...]
    edge_ref[pl.ds(pl.multiple_of((1 - odd) * halo, 32), halo), :] = near_ref[...]


def pair_kernel(mine_ref, other_ref, keep_ref, send_ref, total_ref):
    bit = lax.rem(lax.axis_index("elem") // 2, 2)
    total_ref[...] = mine_ref[...] + other_ref[...]
    half = total_ref.shape[0] // 2
    keep_ref[...] = total_ref[pl.ds(pl.multiple_of(bit * half, 8), half), :]
    send_ref[...] = total_ref[pl.ds(pl.multiple_of((1 - bit) * half, 8), half), :].astype(BF)


def add_kernel(mine_ref, other_ref, total_ref, send_ref):
    total = mine_ref[...] + other_ref[...].astype(F32)
    total_ref[...] = total
    send_ref[...] = total.astype(BF)


def split_kernel(a_ref, high_ref, low_ref):
    a = a_ref[...].T
    high = a.astype(BF)
    high_ref[...] = high
    low_ref[...] = (a - high.astype(F32)).astype(BF)


def admit_kernel(count, mine_ref, *refs):
    others, (high_ref, low_ref, adj_ref) = refs[:count], refs[count:]
    total = mine_ref[...]
    for other in others:
        total += other[...].astype(F32)
    high = total.astype(BF)
    low = (total - high.astype(F32)).astype(BF)
    both = lax.dot_general(
        jnp.concatenate([high, low], axis=0), high_ref[...], NN, preferred_element_type=F32
    )
    rows = mine_ref.shape[0]
    adj = both[:rows] + both[rows:]
    adj += lax.dot_general(high, low_ref[...], NN, preferred_element_type=F32)
    adj_ref[...] = adj.astype(BF)


def back_kernel(
    own_ref, y_ref, core_ref, both_ref, modes_ref, mid_ref, edge_ref, adj_hbm, sens_hbm,
    adj_ref, sens_ref, field_ref, sems,
):
    me = lax.axis_index("elem")
    odd = lax.rem(me, 2)
    bit = lax.rem(me // 2, 2)
    quarter = own_ref.shape[0]
    for ref, c, y in (
        (own_ref, odd, bit),
        (y_ref, odd, 1 - bit),
        (core_ref, 1 - odd, bit),
        (both_ref, 1 - odd, 1 - bit),
    ):
        at = pl.multiple_of((2 * c + y) * quarter, 16)
        field_ref[pl.ds(at, quarter), :] = ref[...]
    field = field_ref[...]
    elem_rows = modes_ref.shape[0]
    halo = edge_ref.shape[0] // 2
    last = elem_rows - halo
    leaving = []
    for k in range(elem_rows // CHUNK):
        at = k * CHUNK
        part = lax.dot_general(
            modes_ref[at : at + CHUNK, :], field, NT, preferred_element_type=F32
        )
        adj_ref[at : at + CHUNK, :] = part.astype(BF)
        rows = pl.ds(at, CHUNK)
        leaving.append(pltpu.make_async_copy(adj_ref.at[rows], adj_hbm.at[rows], sems.at[k]))
        leaving[-1].start()
        if at < halo:
            st = edge_ref[at : at + CHUNK, :]
        elif at < last:
            st = mid_ref[at - halo : at - halo + CHUNK, :]
        else:
            st = edge_ref[at - last + halo : at - last + halo + CHUNK, :]
        product = part * st.astype(F32)
        for i in range(CHUNK // LANES):
            row = jnp.sum(product[i * LANES : (i + 1) * LANES, :].T, axis=0, keepdims=True)
            sens_ref[at // LANES + i : at // LANES + i + 1, :] = row
    leaving.append(pltpu.make_async_copy(sens_ref, sens_hbm, sems.at[elem_rows // CHUNK]))
    leaving[-1].start()
    for copy in leaving:
        copy.wait()


def body(records, panel_owner, panel_slot, stiff_blocks, block_cols, modes, admittance):
    owners = lax.axis_size("elem")
    chips = owners // 2
    pan, width = records.shape
    cap = 2 * pan // owners
    share = LANES // cap
    elem_rows, mode_count = modes.shape
    blocks, nnz, size, _ = stiff_blocks.shape
    halo = REACH * size
    message = (chips, cap + TAIL, width)

    def swap(array, mask):
        return lax.ppermute(array, "elem", [(i, i ^ mask) for i in range(owners)])

    def swap_far(array):
        pairs = [(i, i + 1) for i in range(1, owners - 1, 2)]
        return lax.ppermute(array, "elem", pairs + [(j, i) for i, j in pairs])

    def turn(array, dz, dy):
        pairs = []
        for i in range(owners):
            z, y, core = i // 4, i // 2 % 2, i % 2
            pairs.append((i, ((z + dz) % (chips // 2) * 2 + (y + dy) % 2) * 2 + core))
        return lax.ppermute(array, "elem", pairs)

    owner = panel_owner.reshape(1, pan)
    cross, rank, slots, held = call(
        functools.partial(pack_kernel, cap),
        (
            shape(message, BF),
            shape((1, pan), F32),
            shape((share, 2 * owners, LANES), F32),
            shape((pan, width), BF),
        ),
        owner,
        panel_slot.reshape(pan // LANES, LANES),
        records,
        flops=owners * cap * pan * width,
    )
    got_cross = swap(cross, 1)
    own = call(
        functools.partial(pack_own_kernel, cap),
        shape(message, BF),
        owner, rank, slots, held,
        flops=owners * cap * pan * width,
    )
    packed = call(
        functools.partial(merge_kernel, cap),
        (shape((2 * cap + TAIL, width), BF),) * chips,
        own, got_cross,
    )
    offsets = range(1, chips)
    got = {j: turn(packed[j], j // 2, j % 2) for j in offsets}
    got[0] = packed[0]
    total_rows = owners * cap
    far, slot_row, landed = call(
        functools.partial(far_kernel, cap, elem_rows, chips),
        (shape((halo, width), BF), shape((1, total_rows), F32), shape((total_rows, width), BF)),
        *[got[j] for j in range(chips)],
        flops=8 * total_rows * halo * width,
    )
    got_far = swap_far(far)
    near = call(
        functools.partial(near_kernel, elem_rows),
        shape((halo, width), BF),
        slot_row, landed,
        flops=2 * total_rows * halo * width,
    )
    got_near = swap(near, 1)
    cols = block_cols.T
    loads, st_mid = call(
        middle_kernel,
        (shape((elem_rows, width), BF), shape((elem_rows - 2 * halo, width), BF)),
        slot_row, landed, near, far, stiff_blocks, cols,
        smem=(5,),
        flops=4 * total_rows * halo * width,
    )
    extended = pltpu.VMEM((elem_rows + 2 * halo, width), BF)
    st_near, modal_near = call(
        near_rows_kernel,
        (shape((halo, width), BF), shape((width, mode_count), F32)),
        loads, got_near, stiff_blocks, cols, modes, st_mid,
        smem=(3,),
        scratch=(extended,),
        flops=2 * (elem_rows - halo) * width * mode_count,
    )
    st_edge, keep, send = call(
        far_rows_kernel,
        (
            shape((2 * halo, width), BF),
            shape((width // 2, mode_count), F32),
            shape((width // 2, mode_count), F32),
        ),
        loads, got_far, stiff_blocks, cols, modes, st_near, modal_near,
        smem=(3,),
        scratch=(extended, pltpu.VMEM((halo, width), BF), pltpu.VMEM((width, mode_count), F32)),
        flops=2 * halo * width * mode_count,
    )
    quarter = width // 4
    piece = shape((quarter, mode_count), BF)
    keep, send = call(
        pair_kernel,
        (shape((quarter, mode_count), F32), piece),
        keep, swap(send, 1),
        scratch=(pltpu.VMEM((width // 2, mode_count), F32),),
    )
    total, send = call(
        add_kernel, (shape((quarter, mode_count), F32), piece), keep, swap(send, 2)
    )
    groups = chips // 2
    steps = sorted(range(1, groups), key=lambda k: min(k, groups - k))
    others = [turn(send, k, 0) for k in steps]
    a_high, a_low = call(
        split_kernel,
        (shape(admittance.shape, BF), shape(admittance.shape, BF)),
        admittance,
        flops=4 * admittance.size,
    )
    mine = call(
        functools.partial(admit_kernel, len(others)),
        piece,
        total, *others, a_high, a_low,
        flops=6 * quarter * mode_count * mode_count,
    )
    across = swap(mine, 2)
    beside = swap(mine, 1)
    both = swap(across, 1)
    adjoint, sensitivity = call(
        back_kernel,
        (shape((elem_rows, width), BF), shape((elem_rows // LANES, LANES), F32)),
        mine, across, beside, both, modes, st_mid, st_edge,
        out=pltpu.HBM,
        scratch=(
            pltpu.VMEM((elem_rows, width), BF),
            pltpu.VMEM((elem_rows // LANES, LANES), F32),
            pltpu.VMEM((width, mode_count), BF),
            pltpu.SemaphoreType.DMA((elem_rows // CHUNK + 1,)),
        ),
        flops=2 * elem_rows * width * mode_count,
    )
    return adjoint, sensitivity.reshape(elem_rows)


def solution(mesh):
    in_specs = (
        P(("case", "elem"), None),
        P("elem", None),
        P("elem"),
        P("elem", None, None, None),
        P("elem", None),
        P("elem", None),
        P("case", None),
    )
    out_specs = (P(("case", "elem"), None), P(("case", "elem")))
    return jax.shard_map(body, mesh=mesh, in_specs=in_specs, out_specs=out_specs, check_vma=False)
```

```python
import functools

import jax
import jax.numpy as jnp
from jax import lax
from jax.experimental import pallas as pl
from jax.experimental.pallas import tpu as pltpu
from jax.sharding import PartitionSpec as P

LANES = 128
TAIL = 16
REACH = 8
BF = jnp.bfloat16
F32 = jnp.float32
NT = (((1,), (1,)), ((), ()))
NN = (((1,), (0,)), ((), ()))
TN = (((0,), (0,)), ((), ()))


def call(kernel, out_shape, *operands, smem=(), hbm=(), out=pltpu.VMEM, scratch=(), flops=0, limit=16 * 2**20):
    space = [
        pltpu.SMEM if k in smem else pltpu.HBM if k in hbm else pltpu.VMEM
        for k in range(len(operands))
    ]
    moved = sum(x.size * x.dtype.itemsize for x in operands)
    return pl.pallas_call(
        kernel,
        out_shape=out_shape,
        in_specs=[pl.BlockSpec(memory_space=s) for s in space],
        out_specs=jax.tree.map(lambda _: pl.BlockSpec(memory_space=out), out_shape),
        scratch_shapes=list(scratch),
        compiler_params=pltpu.CompilerParams(vmem_limit_bytes=limit),
        cost_estimate=pl.CostEstimate(flops=flops, bytes_accessed=moved, transcendentals=0),
    )(*operands)


def shape(dims, dtype):
    return jax.ShapeDtypeStruct(dims, dtype)


def odd_core():
    return lax.rem(lax.axis_index("elem"), 2)


def hot(rows, key):
    row = lax.broadcasted_iota(jnp.int32, (rows, key.shape[1]), 0).astype(F32).astype(BF)
    return jnp.where(row == key, jnp.ones((), BF), jnp.zeros((), BF))


def write_messages(cross, cap, chips, owner, rank, records, slots_ref, out_ref):
    me = lax.axis_index("elem")
    core = lax.rem(me + cross, 2)
    y, z = lax.rem(me // 2, 2), me // 4
    share, owners = LANES // cap, 2 * chips
    tail_row = lax.broadcasted_iota(jnp.int32, (TAIL, LANES), 0) - 2 * cross
    for j in range(chips):
        dz, dy = j // 2, j % 2
        to = (lax.rem(z + dz, chips // 2) * 2 + lax.rem(y + dy, 2)) * 2 + core
        key = jnp.where(owner == to, rank, -1.0).astype(BF)
        out_ref[j, 0:cap, :] = jnp.dot(
            hot(cap, key), records, preferred_element_type=F32
        ).astype(BF)
        place = (dy * 2 + cross) % share
        high = slots_ref[place, pl.ds(to, 1), :]
        low = slots_ref[place, pl.ds(owners + to, 1), :]
        tail = jnp.where(tail_row == 0, high, jnp.where(tail_row == 1, low, 0.0))
        out_ref[j, cap : cap + TAIL, :] = tail.astype(BF)


def pack_kernel(
    cap, owner_ref, slot_ref, rec_ref, cross_ref, rank_ref, slots_ref, held_ref
):
    pan = rec_ref.shape[0]
    owners = slots_ref.shape[1] // 2
    pieces = pan // LANES
    before = lax.broadcasted_iota(jnp.int32, (LANES, LANES), 0)
    after = lax.broadcasted_iota(jnp.int32, (LANES, LANES), 1)
    triangle = jnp.where(before <= after, 1.0, 0.0).astype(BF)
    owner = owner_ref[...]
    slot = jnp.concatenate([slot_ref[k : k + 1, :] for k in range(pieces)], axis=1)
    held_ref[...] = rec_ref[...]
    match = lax.broadcasted_iota(jnp.int32, (owners, pan), 0) == owner
    match_f = jnp.where(match, 1.0, 0.0)
    stacked = jnp.concatenate(
        [match_f[:, k * LANES : (k + 1) * LANES] for k in range(pieces)], axis=0
    ).astype(BF)
    running = jnp.dot(stacked, triangle, preferred_element_type=F32)
    offset = jnp.zeros((owners, 1), F32)
    ranks = []
    for k in range(pieces):
        piece = running[k * owners : (k + 1) * owners] + offset
        picked = match_f[:, k * LANES : (k + 1) * LANES] * piece
        ranks.append(jnp.sum(picked, axis=0, keepdims=True) - 1.0)
        offset = piece[:, LANES - 1 : LANES]
    rank = jnp.concatenate(ranks, axis=1)
    rank_ref[...] = rank
    high = (slot >> 6).astype(F32)
    low = (slot & 63).astype(F32)
    weights = jnp.concatenate([match_f * high, match_f * low], axis=0).astype(BF)
    for place in range(LANES // cap):
        spread = hot(LANES, (rank + float(place * cap)).astype(BF))
        slots_ref[place] = lax.dot_general(weights, spread, NT, preferred_element_type=F32)
    write_messages(1, cap, owners // 2, owner, rank, rec_ref[...], slots_ref, cross_ref)


def pack_own_kernel(cap, owner_ref, rank_ref, slots_ref, rec_ref, own_ref):
    chips = slots_ref.shape[1] // 4
    write_messages(
        0, cap, chips, owner_ref[...], rank_ref[...], rec_ref[...], slots_ref, own_ref
    )


def merge_kernel(cap, own_ref, cross_ref, *out_refs):
    for j, ref in enumerate(out_refs):
        ref[0:cap] = own_ref[j, 0:cap]
        ref[cap : 2 * cap] = cross_ref[j, 0:cap]
        ref[2 * cap :] = own_ref[j, cap:] + cross_ref[j, cap:]


CHUNK = 256


def loads_at(slots, records, base, rows):
    key = slots - base.astype(F32)
    key = jnp.where((key >= 0.0) & (key < float(rows)), key, -1.0).astype(BF)
    return jnp.dot(hot(rows, key), records, preferred_element_type=F32)


def land(cap, got_refs, records_ref):
    share = LANES // cap
    order = [(ref, x) for ref in got_refs for x in range(2)]
    for k, ref in enumerate(got_refs):
        records_ref[2 * k * cap : 2 * (k + 1) * cap, :] = ref[0 : 2 * cap, :]
    rows = []
    for group in range(len(order) // share):
        row = None
        for ref, x in order[group * share : (group + 1) * share]:
            tail = ref[2 * cap :, :].astype(F32)
            part = tail[2 * x : 2 * x + 1] * 64.0 + tail[2 * x + 1 : 2 * x + 2]
            row = part if row is None else row + part
        rows.append(row)
    return jnp.concatenate(rows, axis=1)


def early_kernel(cap, count, *refs):
    got_refs, (sum_ref, records_ref) = refs[:count], refs[count:]
    slots = land(cap, got_refs, records_ref)
    records = records_ref[...]
    for k in range(sum_ref.shape[0] // CHUNK):
        at = k * CHUNK
        sum_ref[at : at + CHUNK, :] = loads_at(slots, records, jnp.int32(at), CHUNK)


def far_kernel(cap, count, *refs):
    got_refs, (sum_ref, far_ref, slots_ref, records_ref) = refs[:count], refs[count:]
    slots = land(cap, got_refs, records_ref)
    slots_ref[...] = slots
    halo = far_ref.shape[0]
    first = jnp.where(odd_core() == 1, sum_ref.shape[0] - halo, 0)
    records = records_ref[...]
    for k in range(halo // CHUNK):
        base = first + k * CHUNK
        start = sum_ref[pl.ds(pl.multiple_of(base, CHUNK), CHUNK), :]
        far_ref[k * CHUNK : (k + 1) * CHUNK, :] = (
            start + loads_at(slots, records, base, CHUNK)
        ).astype(BF)


def near_kernel(sum_ref, slots_ref, records_ref, near_ref):
    halo = near_ref.shape[0]
    first = jnp.where(odd_core() == 1, 0, sum_ref.shape[0] - halo)
    for k in range(halo // CHUNK):
        base = first + k * CHUNK
        start = sum_ref[pl.ds(pl.multiple_of(base, CHUNK), CHUNK), :]
        near_ref[k * CHUNK : (k + 1) * CHUNK, :] = (
            start + loads_at(slots_ref[...], records_ref[...], base, CHUNK)
        ).astype(BF)


def stiffen(stiff_ref, cols_ref, loads_ref, block, first_col):
    size = stiff_ref.shape[2]
    total = None
    for j in range(stiff_ref.shape[1]):
        start = pl.multiple_of((cols_ref[j, block] - first_col) * size, 32)
        part = jnp.dot(
            stiff_ref[block, j], loads_ref[pl.ds(start, size), :], preferred_element_type=F32
        )
        total = part if total is None else total + part
    return total.astype(BF)


def middle_kernel(
    sum_ref, slots_ref, records_ref, near_ref, far_ref, stiff_ref, cols_ref, loads_ref, st_ref
):
    elem_rows = loads_ref.shape[0]
    halo = near_ref.shape[0]
    blocks, _, size, _ = stiff_ref.shape
    odd = odd_core()
    last = elem_rows - halo
    near_at = pl.multiple_of(jnp.where(odd == 1, 0, last), 32)
    far_at = pl.multiple_of(jnp.where(odd == 1, last, 0), 32)
    loads_ref[pl.ds(near_at, halo), :] = near_ref[...]
    loads_ref[pl.ds(far_at, halo), :] = far_ref[...]
    for k in range((last - halo) // CHUNK):
        base = halo + k * CHUNK
        loads_ref[base : base + CHUNK, :] = (
            sum_ref[base : base + CHUNK, :]
            + loads_at(slots_ref[...], records_ref[...], jnp.int32(base), CHUNK)
        ).astype(BF)
    first_col = lax.axis_index("elem") * blocks
    for b in range(REACH, blocks - REACH):
        st_ref[(b - REACH) * size : (b - REACH + 1) * size, :] = stiffen(
            stiff_ref, cols_ref, loads_ref, b, first_col
        )


def outer_rows(side, loads_ref, got_ref, stiff_ref, cols_ref, st_ref, ext_ref):
    halo = got_ref.shape[0]
    blocks, _, size, _ = stiff_ref.shape
    end = halo + loads_ref.shape[0]
    got_at = pl.multiple_of(side * end, 32)
    ext_ref[halo:end, :] = loads_ref[...]
    ext_ref[pl.ds(got_at, halo), :] = got_ref[...]
    first_col = lax.axis_index("elem") * blocks - REACH
    for k in range(REACH):
        st_ref[k * size : (k + 1) * size, :] = stiffen(
            stiff_ref, cols_ref, ext_ref, side * (blocks - REACH) + k, first_col
        )


def near_rows_kernel(
    loads_ref, got_ref, stiff_ref, cols_ref, modes_ref, mid_ref, st_ref, modal_ref, ext_ref
):
    side = 1 - odd_core()
    outer_rows(side, loads_ref, got_ref, stiff_ref, cols_ref, st_ref, ext_ref)
    halo = got_ref.shape[0]
    last = modes_ref.shape[0] - halo
    at = pl.multiple_of(side * last, 32)
    modal_ref[...] = lax.dot_general(
        mid_ref[...], modes_ref[halo:last, :], TN, preferred_element_type=F32
    ) + lax.dot_general(
        st_ref[...], modes_ref[pl.ds(at, halo), :], TN, preferred_element_type=F32
    )


def far_rows_kernel(
    loads_ref, got_ref, stiff_ref, cols_ref, modes_ref, near_ref, modal_ref,
    edge_ref, keep_ref, send_ref, ext_ref, st_ref, total_ref,
):
    odd = odd_core()
    outer_rows(odd, loads_ref, got_ref, stiff_ref, cols_ref, st_ref, ext_ref)
    halo = got_ref.shape[0]
    last = modes_ref.shape[0] - halo
    at = pl.multiple_of(odd * last, 32)
    total_ref[...] = modal_ref[...] + lax.dot_general(
        st_ref[...], modes_ref[pl.ds(at, halo), :], TN, preferred_element_type=F32
    )
    half = total_ref.shape[0] // 2
    keep_ref[...] = total_ref[pl.ds(pl.multiple_of(odd * half, 8), half), :]
    send_ref[...] = total_ref[pl.ds(pl.multiple_of((1 - odd) * half, 8), half), :]
    edge_ref[pl.ds(pl.multiple_of(odd * halo, 32), halo), :] = st_ref[...]
    edge_ref[pl.ds(pl.multiple_of((1 - odd) * halo, 32), halo), :] = near_ref[...]


def pair_kernel(mine_ref, other_ref, keep_ref, send_ref, total_ref):
    bit = lax.rem(lax.axis_index("elem") // 2, 2)
    total_ref[...] = mine_ref[...] + other_ref[...]
    half = total_ref.shape[0] // 2
    keep_ref[...] = total_ref[pl.ds(pl.multiple_of(bit * half, 8), half), :]
    send_ref[...] = total_ref[pl.ds(pl.multiple_of((1 - bit) * half, 8), half), :].astype(BF)


def add_kernel(mine_ref, other_ref, total_ref, send_ref):
    total = mine_ref[...] + other_ref[...].astype(F32)
    total_ref[...] = total
    send_ref[...] = total.astype(BF)


def split_kernel(a_ref, high_ref, low_ref):
    a = a_ref[...].T
    high = a.astype(BF)
    high_ref[...] = high
    low_ref[...] = (a - high.astype(F32)).astype(BF)


def admit_kernel(count, mine_ref, *refs):
    others, (high_ref, low_ref, adj_ref) = refs[:count], refs[count:]
    total = mine_ref[...]
    for other in others:
        total += other[...].astype(F32)
    high = total.astype(BF)
    low = (total - high.astype(F32)).astype(BF)
    both = lax.dot_general(
        jnp.concatenate([high, low], axis=0), high_ref[...], NN, preferred_element_type=F32
    )
    rows = mine_ref.shape[0]
    adj = both[:rows] + both[rows:]
    adj += lax.dot_general(high, low_ref[...], NN, preferred_element_type=F32)
    adj_ref[...] = adj.astype(BF)


def turn_kernel(modes_ref, mid_ref, edge_ref, modes_t_ref, st_t_ref):
    elem_rows = modes_ref.shape[0]
    halo = edge_ref.shape[0] // 2
    last = elem_rows - halo
    for k in range(elem_rows // CHUNK):
        at = k * CHUNK
        modes_t_ref[:, at : at + CHUNK] = modes_ref[at : at + CHUNK, :].T
    st_t_ref[:, 0:halo] = edge_ref[0:halo, :].T
    st_t_ref[:, halo:last] = mid_ref[...].T
    st_t_ref[:, last:] = edge_ref[halo:, :].T


def back_kernel(
    own_ref, y_ref, core_ref, both_ref, modes_ref, st_ref, adj_hbm, sens_hbm,
    adj_ref, sens_ref, field_ref, sems,
):
    me = lax.axis_index("elem")
    odd = lax.rem(me, 2)
    bit = lax.rem(me // 2, 2)
    quarter = own_ref.shape[0]
    for ref, c, y in (
        (own_ref, odd, bit),
        (y_ref, odd, 1 - bit),
        (core_ref, 1 - odd, bit),
        (both_ref, 1 - odd, 1 - bit),
    ):
        at = pl.multiple_of((2 * c + y) * quarter, 16)
        field_ref[pl.ds(at, quarter), :] = ref[...]
    field = field_ref[...]
    elem_rows = modes_ref.shape[1]
    leaving = []
    for k in range(elem_rows // CHUNK):
        at = k * CHUNK
        part = jnp.dot(field, modes_ref[:, at : at + CHUNK], preferred_element_type=F32)
        row = jnp.sum(part * st_ref[:, at : at + CHUNK].astype(F32), axis=0, keepdims=True)
        for i in range(CHUNK // LANES):
            cols = slice(i * LANES, (i + 1) * LANES)
            adj_ref[at + i * LANES : at + (i + 1) * LANES, :] = part[:, cols].T.astype(BF)
            sens_ref[at // LANES + i : at // LANES + i + 1, :] = row[:, cols]
        rows = pl.ds(at, CHUNK)
        leaving.append(pltpu.make_async_copy(adj_ref.at[rows], adj_hbm.at[rows], sems.at[k]))
        leaving[-1].start()
    leaving.append(pltpu.make_async_copy(sens_ref, sens_hbm, sems.at[elem_rows // CHUNK]))
    leaving[-1].start()
    for copy in leaving:
        copy.wait()


def body(records, panel_owner, panel_slot, stiff_blocks, block_cols, modes, admittance):
    owners = lax.axis_size("elem")
    chips = owners // 2
    pan, width = records.shape
    cap = 2 * pan // owners
    share = LANES // cap
    elem_rows, mode_count = modes.shape
    blocks, nnz, size, _ = stiff_blocks.shape
    halo = REACH * size
    message = (chips, cap + TAIL, width)

    def swap(array, mask):
        return lax.ppermute(array, "elem", [(i, i ^ mask) for i in range(owners)])

    def swap_far(array):
        pairs = [(i, i + 1) for i in range(1, owners - 1, 2)]
        return lax.ppermute(array, "elem", pairs + [(j, i) for i, j in pairs])

    def turn(array, dz, dy):
        pairs = []
        for i in range(owners):
            z, y, core = i // 4, i // 2 % 2, i % 2
            pairs.append((i, ((z + dz) % (chips // 2) * 2 + (y + dy) % 2) * 2 + core))
        return lax.ppermute(array, "elem", pairs)

    owner = panel_owner.reshape(1, pan)
    cross, rank, slots, held = call(
        functools.partial(pack_kernel, cap),
        (
            shape(message, BF),
            shape((1, pan), F32),
            shape((share, 2 * owners, LANES), F32),
            shape((pan, width), BF),
        ),
        owner,
        panel_slot.reshape(pan // LANES, LANES),
        records,
        flops=owners * cap * pan * width,
    )
    got_cross = swap(cross, 1)
    own = call(
        functools.partial(pack_own_kernel, cap),
        shape(message, BF),
        owner, rank, slots, held,
        flops=owners * cap * pan * width,
    )
    packed = call(
        functools.partial(merge_kernel, cap),
        (shape((2 * cap + TAIL, width), BF),) * chips,
        own, got_cross,
    )
    offsets = range(1, chips)
    got = {j: turn(packed[j], j // 2, j % 2) for j in offsets}
    got[0] = packed[0]
    half = chips // 2
    late_rows = half * 2 * cap
    early = call(
        functools.partial(early_kernel, cap, half),
        shape((elem_rows, width), F32),
        *[got[j] for j in range(half)],
        scratch=(pltpu.VMEM((late_rows, width), BF),),
        flops=2 * late_rows * elem_rows * width,
    )
    far, slot_row, landed = call(
        functools.partial(far_kernel, cap, chips - half),
        (shape((halo, width), BF), shape((1, late_rows), F32), shape((late_rows, width), BF)),
        *[got[j] for j in range(half, chips)], early,
        flops=16 * late_rows * halo * width,
    )
    got_far = swap_far(far)
    near = call(
        near_kernel,
        shape((halo, width), BF),
        early, slot_row, landed,
        flops=2 * late_rows * halo * width,
    )
    got_near = swap(near, 1)
    cols = block_cols.T
    loads, st_mid = call(
        middle_kernel,
        (shape((elem_rows, width), BF), shape((elem_rows - 2 * halo, width), BF)),
        early, slot_row, landed, near, far, stiff_blocks, cols,
        smem=(6,),
        flops=4 * late_rows * halo * width,
    )
    extended = pltpu.VMEM((elem_rows + 2 * halo, width), BF)
    st_near, modal_near = call(
        near_rows_kernel,
        (shape((halo, width), BF), shape((width, mode_count), F32)),
        loads, got_near, stiff_blocks, cols, modes, st_mid,
        smem=(3,),
        scratch=(extended,),
        flops=2 * (elem_rows - halo) * width * mode_count,
    )
    st_edge, keep, send = call(
        far_rows_kernel,
        (
            shape((2 * halo, width), BF),
            shape((width // 2, mode_count), F32),
            shape((width // 2, mode_count), F32),
        ),
        loads, got_far, stiff_blocks, cols, modes, st_near, modal_near,
        smem=(3,),
        scratch=(extended, pltpu.VMEM((halo, width), BF), pltpu.VMEM((width, mode_count), F32)),
        flops=2 * halo * width * mode_count,
    )
    quarter = width // 4
    piece = shape((quarter, mode_count), BF)
    keep, send = call(
        pair_kernel,
        (shape((quarter, mode_count), F32), piece),
        keep, swap(send, 1),
        scratch=(pltpu.VMEM((width // 2, mode_count), F32),),
    )
    total, send = call(
        add_kernel, (shape((quarter, mode_count), F32), piece), keep, swap(send, 2)
    )
    groups = chips // 2
    steps = sorted(range(1, groups), key=lambda k: min(k, groups - k))
    others = [turn(send, k, 0) for k in steps]
    a_high, a_low = call(
        split_kernel,
        (shape(admittance.shape, BF), shape(admittance.shape, BF)),
        admittance,
        flops=4 * admittance.size,
    )
    mine = call(
        functools.partial(admit_kernel, len(others)),
        piece,
        total, *others, a_high, a_low,
        flops=6 * quarter * mode_count * mode_count,
    )
    across = swap(mine, 2)
    beside = swap(mine, 1)
    modes_t, st_t = call(
        turn_kernel,
        (shape((mode_count, elem_rows), BF), shape((width, elem_rows), BF)),
        modes, st_mid, st_edge,
    )
    across, modes_t, st_t = lax.optimization_barrier((across, modes_t, st_t))
    both = swap(across, 1)
    adjoint, sensitivity = call(
        back_kernel,
        (shape((elem_rows, width), BF), shape((elem_rows // LANES, LANES), F32)),
        mine, across, beside, both, modes_t, st_t,
        out=pltpu.HBM,
        scratch=(
            pltpu.VMEM((elem_rows, width), BF),
            pltpu.VMEM((elem_rows // LANES, LANES), F32),
            pltpu.VMEM((width, mode_count), BF),
            pltpu.SemaphoreType.DMA((elem_rows // CHUNK + 1,)),
        ),
        flops=2 * elem_rows * width * mode_count,
    )
    return adjoint, sensitivity.reshape(elem_rows)


def solution(mesh):
    in_specs = (
        P(("case", "elem"), None),
        P("elem", None),
        P("elem"),
        P("elem", None, None, None),
        P("elem", None),
        P("elem", None),
        P("case", None),
    )
    out_specs = (P(("case", "elem"), None), P(("case", "elem")))
    return jax.shard_map(body, mesh=mesh, in_specs=in_specs, out_specs=out_specs, check_vma=False)
```

```python
import functools

import jax
import jax.numpy as jnp
from jax import lax
from jax.experimental import pallas as pl
from jax.experimental.pallas import tpu as pltpu
from jax.sharding import PartitionSpec as P

LANES = 128
TAIL = 16
REACH = 8
BF = jnp.bfloat16
F32 = jnp.float32
NT = (((1,), (1,)), ((), ()))
NN = (((1,), (0,)), ((), ()))
TN = (((0,), (0,)), ((), ()))


def call(kernel, out_shape, *operands, smem=(), hbm=(), out=pltpu.VMEM, scratch=(), flops=0, limit=16 * 2**20):
    space = [
        pltpu.SMEM if k in smem else pltpu.HBM if k in hbm else pltpu.VMEM
        for k in range(len(operands))
    ]
    moved = sum(x.size * x.dtype.itemsize for x in operands)
    return pl.pallas_call(
        kernel,
        out_shape=out_shape,
        in_specs=[pl.BlockSpec(memory_space=s) for s in space],
        out_specs=jax.tree.map(lambda _: pl.BlockSpec(memory_space=out), out_shape),
        scratch_shapes=list(scratch),
        compiler_params=pltpu.CompilerParams(vmem_limit_bytes=limit),
        cost_estimate=pl.CostEstimate(flops=flops, bytes_accessed=moved, transcendentals=0),
    )(*operands)


def shape(dims, dtype):
    return jax.ShapeDtypeStruct(dims, dtype)


def odd_core():
    return lax.rem(lax.axis_index("elem"), 2)


def hot(rows, key):
    row = lax.broadcasted_iota(jnp.int32, (rows, key.shape[1]), 0).astype(F32).astype(BF)
    return jnp.where(row == key, jnp.ones((), BF), jnp.zeros((), BF))


def write_messages(cross, cap, chips, owner, rank, records, slots_ref, out_ref):
    me = lax.axis_index("elem")
    core = lax.rem(me + cross, 2)
    y, z = lax.rem(me // 2, 2), me // 4
    share, owners = LANES // cap, 2 * chips
    tail_row = lax.broadcasted_iota(jnp.int32, (TAIL, LANES), 0) - 2 * cross
    for j in range(chips):
        dz, dy = j // 2, j % 2
        to = (lax.rem(z + dz, chips // 2) * 2 + lax.rem(y + dy, 2)) * 2 + core
        key = jnp.where(owner == to, rank, -1.0).astype(BF)
        out_ref[j, 0:cap, :] = jnp.dot(
            hot(cap, key), records, preferred_element_type=F32
        ).astype(BF)
        place = (dy * 2 + cross) % share
        high = slots_ref[place, pl.ds(to, 1), :]
        low = slots_ref[place, pl.ds(owners + to, 1), :]
        tail = jnp.where(tail_row == 0, high, jnp.where(tail_row == 1, low, 0.0))
        out_ref[j, cap : cap + TAIL, :] = tail.astype(BF)


def pack_kernel(
    cap, owner_hbm, slot_hbm, rec_hbm, cross_ref, owner_ref, rank_ref, slots_ref, rec_ref,
    slot_ref, sems,
):
    copies = [
        pltpu.make_async_copy(source, target, sems.at[k])
        for k, (source, target) in enumerate(
            ((owner_hbm, owner_ref), (slot_hbm, slot_ref), (rec_hbm, rec_ref))
        )
    ]
    for copy in copies:
        copy.start()
    pan = rec_ref.shape[0]
    owners = slots_ref.shape[1] // 2
    pieces = pan // LANES
    before = lax.broadcasted_iota(jnp.int32, (LANES, LANES), 0)
    after = lax.broadcasted_iota(jnp.int32, (LANES, LANES), 1)
    triangle = jnp.where(before <= after, 1.0, 0.0).astype(BF)
    copies[0].wait()
    copies[1].wait()
    owner = owner_ref[...]
    slot = jnp.concatenate([slot_ref[k : k + 1, :] for k in range(pieces)], axis=1)
    match = lax.broadcasted_iota(jnp.int32, (owners, pan), 0) == owner
    match_f = jnp.where(match, 1.0, 0.0)
    stacked = jnp.concatenate(
        [match_f[:, k * LANES : (k + 1) * LANES] for k in range(pieces)], axis=0
    ).astype(BF)
    running = jnp.dot(stacked, triangle, preferred_element_type=F32)
    offset = jnp.zeros((owners, 1), F32)
    ranks = []
    for k in range(pieces):
        piece = running[k * owners : (k + 1) * owners] + offset
        picked = match_f[:, k * LANES : (k + 1) * LANES] * piece
        ranks.append(jnp.sum(picked, axis=0, keepdims=True) - 1.0)
        offset = piece[:, LANES - 1 : LANES]
    rank = jnp.concatenate(ranks, axis=1)
    rank_ref[...] = rank
    high = (slot >> 6).astype(F32)
    low = (slot & 63).astype(F32)
    weights = jnp.concatenate([match_f * high, match_f * low], axis=0).astype(BF)
    for place in range(LANES // cap):
        spread = hot(LANES, (rank + float(place * cap)).astype(BF))
        slots_ref[place] = lax.dot_general(weights, spread, NT, preferred_element_type=F32)
    copies[2].wait()
    write_messages(1, cap, owners // 2, owner, rank, rec_ref[...], slots_ref, cross_ref)


def pack_own_kernel(cap, owner_ref, rank_ref, slots_ref, rec_ref, own_ref):
    chips = slots_ref.shape[1] // 4
    write_messages(
        0, cap, chips, owner_ref[...], rank_ref[...], rec_ref[...], slots_ref, own_ref
    )


def merge_kernel(cap, own_ref, cross_ref, *out_refs):
    for j, ref in enumerate(out_refs):
        ref[0:cap] = own_ref[j, 0:cap]
        ref[cap : 2 * cap] = cross_ref[j, 0:cap]
        ref[2 * cap :] = own_ref[j, cap:] + cross_ref[j, cap:]


CHUNK = 256


def loads_at(slots, records, base, rows):
    key = slots - base.astype(F32)
    key = jnp.where((key >= 0.0) & (key < float(rows)), key, -1.0).astype(BF)
    return jnp.dot(hot(rows, key), records, preferred_element_type=F32)


def land(cap, got_refs, records_ref):
    share = LANES // cap
    order = [(ref, x) for ref in got_refs for x in range(2)]
    for k, ref in enumerate(got_refs):
        records_ref[2 * k * cap : 2 * (k + 1) * cap, :] = ref[0 : 2 * cap, :]
    rows = []
    for group in range(len(order) // share):
        row = None
        for ref, x in order[group * share : (group + 1) * share]:
            tail = ref[2 * cap :, :].astype(F32)
            part = tail[2 * x : 2 * x + 1] * 64.0 + tail[2 * x + 1 : 2 * x + 2]
            row = part if row is None else row + part
        rows.append(row)
    return jnp.concatenate(rows, axis=1)


def early_kernel(cap, count, *refs):
    got_refs, (sum_ref, records_ref) = refs[:count], refs[count:]
    slots = land(cap, got_refs, records_ref)
    records = records_ref[...]
    for k in range(sum_ref.shape[0] // CHUNK):
        at = k * CHUNK
        sum_ref[at : at + CHUNK, :] = loads_at(slots, records, jnp.int32(at), CHUNK)


def far_kernel(cap, count, *refs):
    got_refs, (sum_ref, far_ref, slots_ref, records_ref) = refs[:count], refs[count:]
    slots = land(cap, got_refs, records_ref)
    slots_ref[...] = slots
    halo = far_ref.shape[0]
    first = jnp.where(odd_core() == 1, sum_ref.shape[0] - halo, 0)
    records = records_ref[...]
    for k in range(halo // CHUNK):
        base = first + k * CHUNK
        start = sum_ref[pl.ds(pl.multiple_of(base, CHUNK), CHUNK), :]
        far_ref[k * CHUNK : (k + 1) * CHUNK, :] = (
            start + loads_at(slots, records, base, CHUNK)
        ).astype(BF)


def near_kernel(sum_ref, slots_ref, records_ref, near_ref):
    halo = near_ref.shape[0]
    first = jnp.where(odd_core() == 1, 0, sum_ref.shape[0] - halo)
    for k in range(halo // CHUNK):
        base = first + k * CHUNK
        start = sum_ref[pl.ds(pl.multiple_of(base, CHUNK), CHUNK), :]
        near_ref[k * CHUNK : (k + 1) * CHUNK, :] = (
            start + loads_at(slots_ref[...], records_ref[...], base, CHUNK)
        ).astype(BF)


def stiffen(stiff_ref, cols_ref, loads_ref, block, first_col):
    size = stiff_ref.shape[2]
    total = None
    for j in range(stiff_ref.shape[1]):
        start = pl.multiple_of((cols_ref[j, block] - first_col) * size, 32)
        part = jnp.dot(
            stiff_ref[block, j], loads_ref[pl.ds(start, size), :], preferred_element_type=F32
        )
        total = part if total is None else total + part
    return total.astype(BF)


def middle_kernel(
    sum_ref, slots_ref, records_ref, near_ref, far_ref, stiff_ref, cols_ref, loads_ref, st_ref
):
    elem_rows = loads_ref.shape[0]
    halo = near_ref.shape[0]
    blocks, _, size, _ = stiff_ref.shape
    odd = odd_core()
    last = elem_rows - halo
    near_at = pl.multiple_of(jnp.where(odd == 1, 0, last), 32)
    far_at = pl.multiple_of(jnp.where(odd == 1, last, 0), 32)
    loads_ref[pl.ds(near_at, halo), :] = near_ref[...]
    loads_ref[pl.ds(far_at, halo), :] = far_ref[...]
    for k in range((last - halo) // CHUNK):
        base = halo + k * CHUNK
        loads_ref[base : base + CHUNK, :] = (
            sum_ref[base : base + CHUNK, :]
            + loads_at(slots_ref[...], records_ref[...], jnp.int32(base), CHUNK)
        ).astype(BF)
    first_col = lax.axis_index("elem") * blocks
    for b in range(REACH, blocks - REACH):
        st_ref[(b - REACH) * size : (b - REACH + 1) * size, :] = stiffen(
            stiff_ref, cols_ref, loads_ref, b, first_col
        )


def outer_rows(side, loads_ref, got_ref, stiff_ref, cols_ref, st_ref, ext_ref):
    halo = got_ref.shape[0]
    blocks, _, size, _ = stiff_ref.shape
    end = halo + loads_ref.shape[0]
    got_at = pl.multiple_of(side * end, 32)
    ext_ref[halo:end, :] = loads_ref[...]
    ext_ref[pl.ds(got_at, halo), :] = got_ref[...]
    first_col = lax.axis_index("elem") * blocks - REACH
    for k in range(REACH):
        st_ref[k * size : (k + 1) * size, :] = stiffen(
            stiff_ref, cols_ref, ext_ref, side * (blocks - REACH) + k, first_col
        )


def near_rows_kernel(
    loads_ref, got_ref, stiff_ref, cols_ref, modes_ref, mid_ref, st_ref, modal_ref, ext_ref
):
    side = 1 - odd_core()
    outer_rows(side, loads_ref, got_ref, stiff_ref, cols_ref, st_ref, ext_ref)
    halo = got_ref.shape[0]
    last = modes_ref.shape[0] - halo
    at = pl.multiple_of(side * last, 32)
    modal_ref[...] = lax.dot_general(
        mid_ref[...], modes_ref[halo:last, :], TN, preferred_element_type=F32
    ) + lax.dot_general(
        st_ref[...], modes_ref[pl.ds(at, halo), :], TN, preferred_element_type=F32
    )


def far_rows_kernel(
    loads_ref, got_ref, stiff_ref, cols_ref, modes_ref, near_ref, modal_ref,
    edge_ref, keep_ref, send_ref, ext_ref, st_ref, total_ref,
):
    odd = odd_core()
    outer_rows(odd, loads_ref, got_ref, stiff_ref, cols_ref, st_ref, ext_ref)
    halo = got_ref.shape[0]
    last = modes_ref.shape[0] - halo
    at = pl.multiple_of(odd * last, 32)
    total_ref[...] = modal_ref[...] + lax.dot_general(
        st_ref[...], modes_ref[pl.ds(at, halo), :], TN, preferred_element_type=F32
    )
    half = total_ref.shape[0] // 2
    keep_ref[...] = total_ref[pl.ds(pl.multiple_of(odd * half, 8), half), :]
    send_ref[...] = total_ref[pl.ds(pl.multiple_of((1 - odd) * half, 8), half), :]
    edge_ref[pl.ds(pl.multiple_of(odd * halo, 32), halo), :] = st_ref[...]
    edge_ref[pl.ds(pl.multiple_of((1 - odd) * halo, 32), halo), :] = near_ref[...]


def pair_kernel(mine_ref, other_ref, keep_ref, send_ref, total_ref):
    bit = lax.rem(lax.axis_index("elem") // 2, 2)
    total_ref[...] = mine_ref[...] + other_ref[...]
    half = total_ref.shape[0] // 2
    keep_ref[...] = total_ref[pl.ds(pl.multiple_of(bit * half, 8), half), :]
    send_ref[...] = total_ref[pl.ds(pl.multiple_of((1 - bit) * half, 8), half), :].astype(BF)


def add_kernel(mine_ref, other_ref, total_ref, send_ref):
    total = mine_ref[...] + other_ref[...].astype(F32)
    total_ref[...] = total
    send_ref[...] = total.astype(BF)


def split_kernel(a_ref, high_ref, low_ref):
    a = a_ref[...].T
    high = a.astype(BF)
    high_ref[...] = high
    low_ref[...] = (a - high.astype(F32)).astype(BF)


def admit_kernel(count, mine_ref, *refs):
    others, (high_ref, low_ref, adj_ref) = refs[:count], refs[count:]
    total = mine_ref[...]
    for other in others:
        total += other[...].astype(F32)
    high = total.astype(BF)
    low = (total - high.astype(F32)).astype(BF)
    both = lax.dot_general(
        jnp.concatenate([high, low], axis=0), high_ref[...], NN, preferred_element_type=F32
    )
    rows = mine_ref.shape[0]
    adj = both[:rows] + both[rows:]
    adj += lax.dot_general(high, low_ref[...], NN, preferred_element_type=F32)
    adj_ref[...] = adj.astype(BF)


def turn_kernel(modes_ref, mid_ref, edge_ref, modes_t_ref, st_t_ref):
    elem_rows = modes_ref.shape[0]
    halo = edge_ref.shape[0] // 2
    last = elem_rows - halo
    for k in range(elem_rows // CHUNK):
        at = k * CHUNK
        modes_t_ref[:, at : at + CHUNK] = modes_ref[at : at + CHUNK, :].T
    st_t_ref[:, 0:halo] = edge_ref[0:halo, :].T
    st_t_ref[:, halo:last] = mid_ref[...].T
    st_t_ref[:, last:] = edge_ref[halo:, :].T


def back_kernel(
    own_ref, y_ref, core_ref, both_ref, modes_ref, st_ref, adj_hbm, sens_hbm,
    adj_ref, sens_ref, field_ref, sems,
):
    me = lax.axis_index("elem")
    odd = lax.rem(me, 2)
    bit = lax.rem(me // 2, 2)
    quarter = own_ref.shape[0]
    for ref, c, y in (
        (own_ref, odd, bit),
        (y_ref, odd, 1 - bit),
        (core_ref, 1 - odd, bit),
        (both_ref, 1 - odd, 1 - bit),
    ):
        at = pl.multiple_of((2 * c + y) * quarter, 16)
        field_ref[pl.ds(at, quarter), :] = ref[...]
    field = field_ref[...]
    elem_rows = modes_ref.shape[1]
    leaving = []
    for k in range(elem_rows // CHUNK):
        at = k * CHUNK
        part = jnp.dot(field, modes_ref[:, at : at + CHUNK], preferred_element_type=F32)
        row = jnp.sum(part * st_ref[:, at : at + CHUNK].astype(F32), axis=0, keepdims=True)
        for i in range(CHUNK // LANES):
            cols = slice(i * LANES, (i + 1) * LANES)
            adj_ref[at + i * LANES : at + (i + 1) * LANES, :] = part[:, cols].T.astype(BF)
            sens_ref[at // LANES + i : at // LANES + i + 1, :] = row[:, cols]
        rows = pl.ds(at, CHUNK)
        leaving.append(pltpu.make_async_copy(adj_ref.at[rows], adj_hbm.at[rows], sems.at[k]))
        leaving[-1].start()
    leaving.append(pltpu.make_async_copy(sens_ref, sens_hbm, sems.at[elem_rows // CHUNK]))
    leaving[-1].start()
    for copy in leaving:
        copy.wait()


def body(records, panel_owner, panel_slot, stiff_blocks, block_cols, modes, admittance):
    owners = lax.axis_size("elem")
    chips = owners // 2
    pan, width = records.shape
    cap = 2 * pan // owners
    share = LANES // cap
    elem_rows, mode_count = modes.shape
    blocks, nnz, size, _ = stiff_blocks.shape
    halo = REACH * size
    message = (chips, cap + TAIL, width)

    def stay(array):
        return pltpu.with_memory_space_constraint(array, pltpu.HBM)

    def swap(array, mask):
        return lax.ppermute(array, "elem", [(i, i ^ mask) for i in range(owners)])

    def swap_far(array):
        pairs = [(i, i + 1) for i in range(1, owners - 1, 2)]
        return lax.ppermute(array, "elem", pairs + [(j, i) for i, j in pairs])

    def turn(array, dz, dy):
        pairs = []
        for i in range(owners):
            z, y, core = i // 4, i // 2 % 2, i % 2
            pairs.append((i, ((z + dz) % (chips // 2) * 2 + (y + dy) % 2) * 2 + core))
        return lax.ppermute(array, "elem", pairs)

    cross, owner, rank, slots, held = call(
        functools.partial(pack_kernel, cap),
        (
            shape(message, BF),
            shape((1, pan), jnp.int32),
            shape((1, pan), F32),
            shape((share, 2 * owners, LANES), F32),
            shape((pan, width), BF),
        ),
        stay(panel_owner.reshape(1, pan)),
        stay(panel_slot.reshape(pan // LANES, LANES)),
        stay(records),
        hbm=(0, 1, 2),
        scratch=(
            pltpu.VMEM((pan // LANES, LANES), jnp.int32),
            pltpu.SemaphoreType.DMA((3,)),
        ),
        flops=owners * cap * pan * width,
    )
    got_cross = swap(cross, 1)
    own = call(
        functools.partial(pack_own_kernel, cap),
        shape(message, BF),
        owner, rank, slots, held,
        flops=owners * cap * pan * width,
    )
    packed = call(
        functools.partial(merge_kernel, cap),
        (shape((2 * cap + TAIL, width), BF),) * chips,
        own, got_cross,
    )
    offsets = range(1, chips)
    got = {j: turn(packed[j], j // 2, j % 2) for j in offsets}
    got[0] = packed[0]
    half = chips // 2
    late_rows = half * 2 * cap
    early = call(
        functools.partial(early_kernel, cap, half),
        shape((elem_rows, width), F32),
        *[got[j] for j in range(half)],
        scratch=(pltpu.VMEM((late_rows, width), BF),),
        flops=2 * late_rows * elem_rows * width,
    )
    far, slot_row, landed = call(
        functools.partial(far_kernel, cap, chips - half),
        (shape((halo, width), BF), shape((1, late_rows), F32), shape((late_rows, width), BF)),
        *[got[j] for j in range(half, chips)], early,
        flops=16 * late_rows * halo * width,
    )
    got_far = swap_far(far)
    near = call(
        near_kernel,
        shape((halo, width), BF),
        early, slot_row, landed,
        flops=2 * late_rows * halo * width,
    )
    got_near = swap(near, 1)
    cols = block_cols.T
    loads, st_mid = call(
        middle_kernel,
        (shape((elem_rows, width), BF), shape((elem_rows - 2 * halo, width), BF)),
        early, slot_row, landed, near, far, stiff_blocks, cols,
        smem=(6,),
        flops=4 * late_rows * halo * width,
    )
    extended = pltpu.VMEM((elem_rows + 2 * halo, width), BF)
    st_near, modal_near = call(
        near_rows_kernel,
        (shape((halo, width), BF), shape((width, mode_count), F32)),
        loads, got_near, stiff_blocks, cols, modes, st_mid,
        smem=(3,),
        scratch=(extended,),
        flops=2 * (elem_rows - halo) * width * mode_count,
    )
    st_edge, keep, send = call(
        far_rows_kernel,
        (
            shape((2 * halo, width), BF),
            shape((width // 2, mode_count), F32),
            shape((width // 2, mode_count), F32),
        ),
        loads, got_far, stiff_blocks, cols, modes, st_near, modal_near,
        smem=(3,),
        scratch=(extended, pltpu.VMEM((halo, width), BF), pltpu.VMEM((width, mode_count), F32)),
        flops=2 * halo * width * mode_count,
    )
    quarter = width // 4
    piece = shape((quarter, mode_count), BF)
    keep, send = call(
        pair_kernel,
        (shape((quarter, mode_count), F32), piece),
        keep, swap(send, 1),
        scratch=(pltpu.VMEM((width // 2, mode_count), F32),),
    )
    total, send = call(
        add_kernel, (shape((quarter, mode_count), F32), piece), keep, swap(send, 2)
    )
    groups = chips // 2
    steps = sorted(range(1, groups), key=lambda k: min(k, groups - k))
    others = [turn(send, k, 0) for k in steps]
    a_high, a_low = call(
        split_kernel,
        (shape(admittance.shape, BF), shape(admittance.shape, BF)),
        admittance,
        flops=4 * admittance.size,
    )
    mine = call(
        functools.partial(admit_kernel, len(others)),
        piece,
        total, *others, a_high, a_low,
        flops=6 * quarter * mode_count * mode_count,
    )
    across = swap(mine, 2)
    beside = swap(mine, 1)
    modes_t, st_t = call(
        turn_kernel,
        (shape((mode_count, elem_rows), BF), shape((width, elem_rows), BF)),
        modes, st_mid, st_edge,
    )
    across, modes_t, st_t = lax.optimization_barrier((across, modes_t, st_t))
    both = swap(across, 1)
    adjoint, sensitivity = call(
        back_kernel,
        (shape((elem_rows, width), BF), shape((elem_rows // LANES, LANES), F32)),
        mine, across, beside, both, modes_t, st_t,
        out=pltpu.HBM,
        scratch=(
            pltpu.VMEM((elem_rows, width), BF),
            pltpu.VMEM((elem_rows // LANES, LANES), F32),
            pltpu.VMEM((width, mode_count), BF),
            pltpu.SemaphoreType.DMA((elem_rows // CHUNK + 1,)),
        ),
        flops=2 * elem_rows * width * mode_count,
    )
    return adjoint, sensitivity.reshape(elem_rows)


def solution(mesh):
    in_specs = (
        P(("case", "elem"), None),
        P("elem", None),
        P("elem"),
        P("elem", None, None, None),
        P("elem", None),
        P("elem", None),
        P("case", None),
    )
    out_specs = (P(("case", "elem"), None), P(("case", "elem")))
    return jax.shard_map(body, mesh=mesh, in_specs=in_specs, out_specs=out_specs, check_vma=False)
```

```python
import functools

import jax
import jax.numpy as jnp
from jax import lax
from jax.experimental import pallas as pl
from jax.experimental.pallas import tpu as pltpu
from jax.sharding import PartitionSpec as P

LANES = 128
TAIL = 16
REACH = 8
BF = jnp.bfloat16
F32 = jnp.float32
NT = (((1,), (1,)), ((), ()))
NN = (((1,), (0,)), ((), ()))
TN = (((0,), (0,)), ((), ()))


def call(kernel, out_shape, *operands, smem=(), hbm=(), out=pltpu.VMEM, scratch=(), flops=0, limit=16 * 2**20):
    space = [
        pltpu.SMEM if k in smem else pltpu.HBM if k in hbm else pltpu.VMEM
        for k in range(len(operands))
    ]
    moved = sum(x.size * x.dtype.itemsize for x in operands)
    return pl.pallas_call(
        kernel,
        out_shape=out_shape,
        in_specs=[pl.BlockSpec(memory_space=s) for s in space],
        out_specs=jax.tree.map(lambda _: pl.BlockSpec(memory_space=out), out_shape),
        scratch_shapes=list(scratch),
        compiler_params=pltpu.CompilerParams(vmem_limit_bytes=limit),
        cost_estimate=pl.CostEstimate(flops=flops, bytes_accessed=moved, transcendentals=0),
    )(*operands)


def shape(dims, dtype):
    return jax.ShapeDtypeStruct(dims, dtype)


def odd_core():
    return lax.rem(lax.axis_index("elem"), 2)


def hot(rows, key):
    row = lax.broadcasted_iota(jnp.int32, (rows, key.shape[1]), 0).astype(F32).astype(BF)
    return jnp.where(row == key, jnp.ones((), BF), jnp.zeros((), BF))


def write_messages(cross, cap, chips, owner, rank, records, slots_ref, out_ref):
    me = lax.axis_index("elem")
    core = lax.rem(me + cross, 2)
    y, z = lax.rem(me // 2, 2), me // 4
    share, owners = LANES // cap, 2 * chips
    tail_row = lax.broadcasted_iota(jnp.int32, (TAIL, LANES), 0) - 2 * cross
    for j in range(chips):
        dz, dy = j // 2, j % 2
        to = (lax.rem(z + dz, chips // 2) * 2 + lax.rem(y + dy, 2)) * 2 + core
        key = jnp.where(owner == to, rank, -1.0).astype(BF)
        out_ref[j, 0:cap, :] = jnp.dot(
            hot(cap, key), records, preferred_element_type=F32
        ).astype(BF)
        place = (dy * 2 + cross) % share
        high = slots_ref[place, pl.ds(to, 1), :]
        low = slots_ref[place, pl.ds(owners + to, 1), :]
        tail = jnp.where(tail_row == 0, high, jnp.where(tail_row == 1, low, 0.0))
        out_ref[j, cap : cap + TAIL, :] = tail.astype(BF)


def pack_kernel(
    cap, owner_hbm, slot_hbm, rec_hbm, cross_ref, owner_ref, rank_ref, slots_ref, rec_ref,
    slot_ref, sems,
):
    copies = [
        pltpu.make_async_copy(source, target, sems.at[k])
        for k, (source, target) in enumerate(
            ((owner_hbm, owner_ref), (slot_hbm, slot_ref), (rec_hbm, rec_ref))
        )
    ]
    for copy in copies:
        copy.start()
    pan = rec_ref.shape[0]
    owners = slots_ref.shape[1] // 2
    pieces = pan // LANES
    before = lax.broadcasted_iota(jnp.int32, (LANES, LANES), 0)
    after = lax.broadcasted_iota(jnp.int32, (LANES, LANES), 1)
    triangle = jnp.where(before <= after, 1.0, 0.0).astype(BF)
    copies[0].wait()
    copies[1].wait()
    owner = owner_ref[...]
    slot = jnp.concatenate([slot_ref[k : k + 1, :] for k in range(pieces)], axis=1)
    match = lax.broadcasted_iota(jnp.int32, (owners, pan), 0) == owner
    match_f = jnp.where(match, 1.0, 0.0)
    stacked = jnp.concatenate(
        [match_f[:, k * LANES : (k + 1) * LANES] for k in range(pieces)], axis=0
    ).astype(BF)
    running = jnp.dot(stacked, triangle, preferred_element_type=F32)
    offset = jnp.zeros((owners, 1), F32)
    ranks = []
    for k in range(pieces):
        piece = running[k * owners : (k + 1) * owners] + offset
        picked = match_f[:, k * LANES : (k + 1) * LANES] * piece
        ranks.append(jnp.sum(picked, axis=0, keepdims=True) - 1.0)
        offset = piece[:, LANES - 1 : LANES]
    rank = jnp.concatenate(ranks, axis=1)
    rank_ref[...] = rank
    high = (slot >> 6).astype(F32)
    low = (slot & 63).astype(F32)
    weights = jnp.concatenate([match_f * high, match_f * low], axis=0).astype(BF)
    for place in range(LANES // cap):
        spread = hot(LANES, (rank + float(place * cap)).astype(BF))
        slots_ref[place] = lax.dot_general(weights, spread, NT, preferred_element_type=F32)
    copies[2].wait()
    write_messages(1, cap, owners // 2, owner, rank, rec_ref[...], slots_ref, cross_ref)


def pack_own_kernel(cap, owner_ref, rank_ref, slots_ref, rec_ref, own_ref):
    chips = slots_ref.shape[1] // 4
    write_messages(
        0, cap, chips, owner_ref[...], rank_ref[...], rec_ref[...], slots_ref, own_ref
    )


def merge_kernel(cap, own_ref, cross_ref, *out_refs):
    for j, ref in enumerate(out_refs):
        ref[0:cap] = own_ref[j, 0:cap]
        ref[cap : 2 * cap] = cross_ref[j, 0:cap]
        ref[2 * cap :] = own_ref[j, cap:] + cross_ref[j, cap:]


CHUNK = 256


def loads_at(slots, records, base, rows):
    key = slots - base.astype(F32)
    key = jnp.where((key >= 0.0) & (key < float(rows)), key, -1.0).astype(BF)
    return jnp.dot(hot(rows, key), records, preferred_element_type=F32)


def land(cap, got_refs, records_ref):
    share = LANES // cap
    order = [(ref, x) for ref in got_refs for x in range(2)]
    for k, ref in enumerate(got_refs):
        records_ref[2 * k * cap : 2 * (k + 1) * cap, :] = ref[0 : 2 * cap, :]
    rows = []
    for group in range(len(order) // share):
        row = None
        for ref, x in order[group * share : (group + 1) * share]:
            tail = ref[2 * cap :, :].astype(F32)
            part = tail[2 * x : 2 * x + 1] * 64.0 + tail[2 * x + 1 : 2 * x + 2]
            row = part if row is None else row + part
        rows.append(row)
    return jnp.concatenate(rows, axis=1)


def early_kernel(cap, count, *refs):
    got_refs, (sum_ref, records_ref) = refs[:count], refs[count:]
    slots = land(cap, got_refs, records_ref)
    records = records_ref[...]
    for k in range(sum_ref.shape[0] // CHUNK):
        at = k * CHUNK
        sum_ref[at : at + CHUNK, :] = loads_at(slots, records, jnp.int32(at), CHUNK)


def far_kernel(cap, count, *refs):
    got_refs, (sum_ref, far_ref, slots_ref, records_ref) = refs[:count], refs[count:]
    slots = land(cap, got_refs, records_ref)
    slots_ref[...] = slots
    halo = far_ref.shape[0]
    first = jnp.where(odd_core() == 1, sum_ref.shape[0] - halo, 0)
    records = records_ref[...]
    for k in range(halo // CHUNK):
        base = first + k * CHUNK
        start = sum_ref[pl.ds(pl.multiple_of(base, CHUNK), CHUNK), :]
        far_ref[k * CHUNK : (k + 1) * CHUNK, :] = (
            start + loads_at(slots, records, base, CHUNK)
        ).astype(BF)


def near_kernel(sum_ref, slots_ref, records_ref, near_ref):
    halo = near_ref.shape[0]
    first = jnp.where(odd_core() == 1, 0, sum_ref.shape[0] - halo)
    for k in range(halo // CHUNK):
        base = first + k * CHUNK
        start = sum_ref[pl.ds(pl.multiple_of(base, CHUNK), CHUNK), :]
        near_ref[k * CHUNK : (k + 1) * CHUNK, :] = (
            start + loads_at(slots_ref[...], records_ref[...], base, CHUNK)
        ).astype(BF)


def stiffen(stiff_ref, cols_ref, loads_ref, block, first_col):
    size = stiff_ref.shape[2]
    total = None
    for j in range(stiff_ref.shape[1]):
        start = pl.multiple_of((cols_ref[j, block] - first_col) * size, 32)
        part = jnp.dot(
            stiff_ref[block, j], loads_ref[pl.ds(start, size), :], preferred_element_type=F32
        )
        total = part if total is None else total + part
    return total.astype(BF)


def middle_kernel(
    sum_ref, slots_ref, records_ref, near_ref, far_ref, stiff_ref, cols_ref, loads_ref, st_ref
):
    elem_rows = loads_ref.shape[0]
    halo = near_ref.shape[0]
    blocks, _, size, _ = stiff_ref.shape
    odd = odd_core()
    last = elem_rows - halo
    near_at = pl.multiple_of(jnp.where(odd == 1, 0, last), 32)
    far_at = pl.multiple_of(jnp.where(odd == 1, last, 0), 32)
    loads_ref[pl.ds(near_at, halo), :] = near_ref[...]
    loads_ref[pl.ds(far_at, halo), :] = far_ref[...]
    for k in range((last - halo) // CHUNK):
        base = halo + k * CHUNK
        loads_ref[base : base + CHUNK, :] = (
            sum_ref[base : base + CHUNK, :]
            + loads_at(slots_ref[...], records_ref[...], jnp.int32(base), CHUNK)
        ).astype(BF)
    first_col = lax.axis_index("elem") * blocks
    for b in range(REACH, blocks - REACH):
        st_ref[(b - REACH) * size : (b - REACH + 1) * size, :] = stiffen(
            stiff_ref, cols_ref, loads_ref, b, first_col
        )


def outer_rows(side, loads_ref, got_ref, stiff_ref, cols_ref, st_ref, ext_ref):
    halo = got_ref.shape[0]
    blocks, _, size, _ = stiff_ref.shape
    end = halo + loads_ref.shape[0]
    got_at = pl.multiple_of(side * end, 32)
    ext_ref[halo:end, :] = loads_ref[...]
    ext_ref[pl.ds(got_at, halo), :] = got_ref[...]
    first_col = lax.axis_index("elem") * blocks - REACH
    for k in range(REACH):
        st_ref[k * size : (k + 1) * size, :] = stiffen(
            stiff_ref, cols_ref, ext_ref, side * (blocks - REACH) + k, first_col
        )


def near_rows_kernel(
    loads_ref, got_ref, stiff_ref, cols_ref, modes_ref, mid_ref, st_ref, modal_ref, ext_ref
):
    side = 1 - odd_core()
    outer_rows(side, loads_ref, got_ref, stiff_ref, cols_ref, st_ref, ext_ref)
    halo = got_ref.shape[0]
    last = modes_ref.shape[0] - halo
    at = pl.multiple_of(side * last, 32)
    modal_ref[...] = lax.dot_general(
        mid_ref[...], modes_ref[halo:last, :], TN, preferred_element_type=F32
    ) + lax.dot_general(
        st_ref[...], modes_ref[pl.ds(at, halo), :], TN, preferred_element_type=F32
    )


def far_rows_kernel(
    loads_ref, got_ref, stiff_ref, cols_ref, modes_ref, near_ref, modal_ref,
    edge_ref, keep_ref, send_ref, ext_ref, st_ref, total_ref,
):
    odd = odd_core()
    outer_rows(odd, loads_ref, got_ref, stiff_ref, cols_ref, st_ref, ext_ref)
    halo = got_ref.shape[0]
    last = modes_ref.shape[0] - halo
    at = pl.multiple_of(odd * last, 32)
    total_ref[...] = modal_ref[...] + lax.dot_general(
        st_ref[...], modes_ref[pl.ds(at, halo), :], TN, preferred_element_type=F32
    )
    half = total_ref.shape[0] // 2
    keep_ref[...] = total_ref[pl.ds(pl.multiple_of(odd * half, 8), half), :]
    send_ref[...] = total_ref[pl.ds(pl.multiple_of((1 - odd) * half, 8), half), :]
    edge_ref[pl.ds(pl.multiple_of(odd * halo, 32), halo), :] = st_ref[...]
    edge_ref[pl.ds(pl.multiple_of((1 - odd) * halo, 32), halo), :] = near_ref[...]


def pair_kernel(mine_ref, other_ref, keep_ref, send_ref, total_ref):
    bit = lax.rem(lax.axis_index("elem") // 2, 2)
    total_ref[...] = mine_ref[...] + other_ref[...]
    half = total_ref.shape[0] // 2
    keep_ref[...] = total_ref[pl.ds(pl.multiple_of(bit * half, 8), half), :]
    send_ref[...] = total_ref[pl.ds(pl.multiple_of((1 - bit) * half, 8), half), :].astype(BF)


def add_kernel(mine_ref, other_ref, total_ref, send_ref):
    total = mine_ref[...] + other_ref[...].astype(F32)
    total_ref[...] = total
    send_ref[...] = total.astype(BF)


def split_kernel(a_ref, high_ref, low_ref):
    a = a_ref[...].T
    high = a.astype(BF)
    high_ref[...] = high
    low_ref[...] = (a - high.astype(F32)).astype(BF)


def admit_kernel(count, mine_ref, *refs):
    others, (high_ref, low_ref, adj_ref) = refs[:count], refs[count:]
    total = mine_ref[...]
    for other in others:
        total += other[...].astype(F32)
    high = total.astype(BF)
    low = (total - high.astype(F32)).astype(BF)
    both = lax.dot_general(
        jnp.concatenate([high, low], axis=0), high_ref[...], NN, preferred_element_type=F32
    )
    rows = mine_ref.shape[0]
    adj = both[:rows] + both[rows:]
    adj += lax.dot_general(high, low_ref[...], NN, preferred_element_type=F32)
    adj_ref[...] = adj.astype(BF)


def turn_kernel(modes_ref, mid_ref, edge_ref, modes_t_ref, st_t_ref):
    elem_rows = modes_ref.shape[0]
    halo = edge_ref.shape[0] // 2
    last = elem_rows - halo
    for k in range(elem_rows // CHUNK):
        at = k * CHUNK
        modes_t_ref[:, at : at + CHUNK] = modes_ref[at : at + CHUNK, :].T
    st_t_ref[:, 0:halo] = edge_ref[0:halo, :].T
    st_t_ref[:, halo:last] = mid_ref[...].T
    st_t_ref[:, last:] = edge_ref[halo:, :].T


def back_kernel(
    own_ref, y_ref, core_ref, both_ref, modes_ref, st_ref, adj_hbm, sens_hbm,
    adj_ref, sens_ref, field_ref, sems,
):
    me = lax.axis_index("elem")
    odd = lax.rem(me, 2)
    bit = lax.rem(me // 2, 2)
    quarter = own_ref.shape[0]
    for ref, c, y in (
        (own_ref, odd, bit),
        (y_ref, odd, 1 - bit),
        (core_ref, 1 - odd, bit),
        (both_ref, 1 - odd, 1 - bit),
    ):
        at = pl.multiple_of((2 * c + y) * quarter, 16)
        field_ref[pl.ds(at, quarter), :] = ref[...]
    field = field_ref[...]
    elem_rows = modes_ref.shape[1]
    leaving = []
    for k in range(elem_rows // CHUNK):
        at = k * CHUNK
        part = jnp.dot(field, modes_ref[:, at : at + CHUNK], preferred_element_type=F32)
        row = jnp.sum(part * st_ref[:, at : at + CHUNK].astype(F32), axis=0, keepdims=True)
        for i in range(CHUNK // LANES):
            cols = slice(i * LANES, (i + 1) * LANES)
            adj_ref[at + i * LANES : at + (i + 1) * LANES, :] = part[:, cols].T.astype(BF)
            sens_ref[at // LANES + i : at // LANES + i + 1, :] = row[:, cols]
        rows = pl.ds(at, CHUNK)
        leaving.append(pltpu.make_async_copy(adj_ref.at[rows], adj_hbm.at[rows], sems.at[k]))
        leaving[-1].start()
    leaving.append(pltpu.make_async_copy(sens_ref, sens_hbm, sems.at[elem_rows // CHUNK]))
    leaving[-1].start()
    for copy in leaving:
        copy.wait()


def body(records, panel_owner, panel_slot, stiff_blocks, block_cols, modes, admittance):
    owners = lax.axis_size("elem")
    chips = owners // 2
    pan, width = records.shape
    cap = 2 * pan // owners
    share = LANES // cap
    elem_rows, mode_count = modes.shape
    blocks, nnz, size, _ = stiff_blocks.shape
    halo = REACH * size
    message = (chips, cap + TAIL, width)

    def stay(array):
        return pltpu.with_memory_space_constraint(array, pltpu.HBM)

    def swap(array, mask):
        return lax.ppermute(array, "elem", [(i, i ^ mask) for i in range(owners)])

    def swap_far(array):
        pairs = [(i, i + 1) for i in range(1, owners - 1, 2)]
        return lax.ppermute(array, "elem", pairs + [(j, i) for i, j in pairs])

    def turn(array, dz, dy):
        pairs = []
        for i in range(owners):
            z, y, core = i // 4, i // 2 % 2, i % 2
            pairs.append((i, ((z + dz) % (chips // 2) * 2 + (y + dy) % 2) * 2 + core))
        return lax.ppermute(array, "elem", pairs)

    cross, owner, rank, slots, held = call(
        functools.partial(pack_kernel, cap),
        (
            shape(message, BF),
            shape((1, pan), jnp.int32),
            shape((1, pan), F32),
            shape((share, 2 * owners, LANES), F32),
            shape((pan, width), BF),
        ),
        stay(panel_owner.reshape(1, pan)),
        stay(panel_slot.reshape(pan // LANES, LANES)),
        stay(records),
        hbm=(0, 1, 2),
        scratch=(
            pltpu.VMEM((pan // LANES, LANES), jnp.int32),
            pltpu.SemaphoreType.DMA((3,)),
        ),
        flops=owners * cap * pan * width,
    )
    got_cross = swap(cross, 1)
    own = call(
        functools.partial(pack_own_kernel, cap),
        shape(message, BF),
        owner, rank, slots, held,
        flops=owners * cap * pan * width,
    )
    packed = call(
        functools.partial(merge_kernel, cap),
        (shape((2 * cap + TAIL, width), BF),) * chips,
        own, got_cross,
    )
    offsets = list(range(1, chips))
    if share == 1:
        reach = chips // 2
        offsets.sort(key=lambda j: (-(j % 2), -min(j // 2, reach - j // 2), j))
    got = {j: turn(packed[j], j // 2, j % 2) for j in offsets}
    got[0] = packed[0]
    arrival = [0, *offsets]
    half = chips // 2
    late_rows = half * 2 * cap
    early = call(
        functools.partial(early_kernel, cap, half),
        shape((elem_rows, width), F32),
        *[got[j] for j in arrival[:half]],
        scratch=(pltpu.VMEM((late_rows, width), BF),),
        flops=2 * late_rows * elem_rows * width,
    )
    far, slot_row, landed = call(
        functools.partial(far_kernel, cap, chips - half),
        (shape((halo, width), BF), shape((1, late_rows), F32), shape((late_rows, width), BF)),
        *[got[j] for j in arrival[half:]], early,
        flops=16 * late_rows * halo * width,
    )
    got_far = swap_far(far)
    near = call(
        near_kernel,
        shape((halo, width), BF),
        early, slot_row, landed,
        flops=2 * late_rows * halo * width,
    )
    got_near = swap(near, 1)
    cols = block_cols.T
    loads, st_mid = call(
        middle_kernel,
        (shape((elem_rows, width), BF), shape((elem_rows - 2 * halo, width), BF)),
        early, slot_row, landed, near, far, stiff_blocks, cols,
        smem=(6,),
        flops=4 * late_rows * halo * width,
    )
    extended = pltpu.VMEM((elem_rows + 2 * halo, width), BF)
    st_near, modal_near = call(
        near_rows_kernel,
        (shape((halo, width), BF), shape((width, mode_count), F32)),
        loads, got_near, stiff_blocks, cols, modes, st_mid,
        smem=(3,),
        scratch=(extended,),
        flops=2 * (elem_rows - halo) * width * mode_count,
    )
    st_edge, keep, send = call(
        far_rows_kernel,
        (
            shape((2 * halo, width), BF),
            shape((width // 2, mode_count), F32),
            shape((width // 2, mode_count), F32),
        ),
        loads, got_far, stiff_blocks, cols, modes, st_near, modal_near,
        smem=(3,),
        scratch=(extended, pltpu.VMEM((halo, width), BF), pltpu.VMEM((width, mode_count), F32)),
        flops=2 * halo * width * mode_count,
    )
    quarter = width // 4
    piece = shape((quarter, mode_count), BF)
    keep, send = call(
        pair_kernel,
        (shape((quarter, mode_count), F32), piece),
        keep, swap(send, 1),
        scratch=(pltpu.VMEM((width // 2, mode_count), F32),),
    )
    total, send = call(
        add_kernel, (shape((quarter, mode_count), F32), piece), keep, swap(send, 2)
    )
    groups = chips // 2
    steps = sorted(range(1, groups), key=lambda k: min(k, groups - k))
    others = [turn(send, k, 0) for k in steps]
    a_high, a_low = call(
        split_kernel,
        (shape(admittance.shape, BF), shape(admittance.shape, BF)),
        admittance,
        flops=4 * admittance.size,
    )
    mine = call(
        functools.partial(admit_kernel, len(others)),
        piece,
        total, *others, a_high, a_low,
        flops=6 * quarter * mode_count * mode_count,
    )
    across = swap(mine, 2)
    beside = swap(mine, 1)
    modes_t, st_t = call(
        turn_kernel,
        (shape((mode_count, elem_rows), BF), shape((width, elem_rows), BF)),
        modes, st_mid, st_edge,
    )
    across, modes_t, st_t = lax.optimization_barrier((across, modes_t, st_t))
    both = swap(across, 1)
    adjoint, sensitivity = call(
        back_kernel,
        (shape((elem_rows, width), BF), shape((elem_rows // LANES, LANES), F32)),
        mine, across, beside, both, modes_t, st_t,
        out=pltpu.HBM,
        scratch=(
            pltpu.VMEM((elem_rows, width), BF),
            pltpu.VMEM((elem_rows // LANES, LANES), F32),
            pltpu.VMEM((width, mode_count), BF),
            pltpu.SemaphoreType.DMA((elem_rows // CHUNK + 1,)),
        ),
        flops=2 * elem_rows * width * mode_count,
    )
    return adjoint, sensitivity.reshape(elem_rows)


def solution(mesh):
    in_specs = (
        P(("case", "elem"), None),
        P("elem", None),
        P("elem"),
        P("elem", None, None, None),
        P("elem", None),
        P("elem", None),
        P("case", None),
    )
    out_specs = (P(("case", "elem"), None), P(("case", "elem")))
    return jax.shard_map(body, mesh=mesh, in_specs=in_specs, out_specs=out_specs, check_vma=False)
```

```python
import functools

import jax
import jax.numpy as jnp
from jax import lax
from jax.experimental import pallas as pl
from jax.experimental.pallas import tpu as pltpu
from jax.sharding import PartitionSpec as P

LANES = 128
TAIL = 16
REACH = 8
BF = jnp.bfloat16
F32 = jnp.float32
NT = (((1,), (1,)), ((), ()))
NN = (((1,), (0,)), ((), ()))
TN = (((0,), (0,)), ((), ()))


def call(kernel, out_shape, *operands, smem=(), hbm=(), out=pltpu.VMEM, scratch=(), flops=0, limit=16 * 2**20):
    space = [
        pltpu.SMEM if k in smem else pltpu.HBM if k in hbm else pltpu.VMEM
        for k in range(len(operands))
    ]
    moved = sum(x.size * x.dtype.itemsize for x in operands)
    return pl.pallas_call(
        kernel,
        out_shape=out_shape,
        in_specs=[pl.BlockSpec(memory_space=s) for s in space],
        out_specs=jax.tree.map(lambda _: pl.BlockSpec(memory_space=out), out_shape),
        scratch_shapes=list(scratch),
        compiler_params=pltpu.CompilerParams(vmem_limit_bytes=limit),
        cost_estimate=pl.CostEstimate(flops=flops, bytes_accessed=moved, transcendentals=0),
    )(*operands)


def shape(dims, dtype):
    return jax.ShapeDtypeStruct(dims, dtype)


def odd_core():
    return lax.rem(lax.axis_index("elem"), 2)


def hot(rows, key):
    row = lax.broadcasted_iota(jnp.int32, (rows, key.shape[1]), 0).astype(F32).astype(BF)
    return jnp.where(row == key, jnp.ones((), BF), jnp.zeros((), BF))


def write_messages(cross, cap, chips, owner, rank, records, slots_ref, out_ref):
    me = lax.axis_index("elem")
    core = lax.rem(me + cross, 2)
    y, z = lax.rem(me // 2, 2), me // 4
    share, owners = LANES // cap, 2 * chips
    tail_row = lax.broadcasted_iota(jnp.int32, (TAIL, LANES), 0) - 2 * cross
    for j in range(chips):
        dz, dy = j // 2, j % 2
        to = (lax.rem(z + dz, chips // 2) * 2 + lax.rem(y + dy, 2)) * 2 + core
        key = jnp.where(owner == to, rank, -1.0).astype(BF)
        out_ref[j, 0:cap, :] = jnp.dot(
            hot(cap, key), records, preferred_element_type=F32
        ).astype(BF)
        place = (dy * 2 + cross) % share
        high = slots_ref[place, pl.ds(to, 1), :]
        low = slots_ref[place, pl.ds(owners + to, 1), :]
        tail = jnp.where(tail_row == 0, high, jnp.where(tail_row == 1, low, 0.0))
        out_ref[j, cap : cap + TAIL, :] = tail.astype(BF)


def pack_kernel(
    cap, owner_hbm, slot_hbm, rec_hbm, cross_ref, owner_ref, rank_ref, slots_ref, rec_ref,
    slot_ref, sems,
):
    copies = [
        pltpu.make_async_copy(source, target, sems.at[k])
        for k, (source, target) in enumerate(
            ((owner_hbm, owner_ref), (slot_hbm, slot_ref), (rec_hbm, rec_ref))
        )
    ]
    for copy in copies:
        copy.start()
    pan = rec_ref.shape[0]
    owners = slots_ref.shape[1] // 2
    pieces = pan // LANES
    before = lax.broadcasted_iota(jnp.int32, (LANES, LANES), 0)
    after = lax.broadcasted_iota(jnp.int32, (LANES, LANES), 1)
    triangle = jnp.where(before <= after, 1.0, 0.0).astype(BF)
    copies[0].wait()
    copies[1].wait()
    owner = owner_ref[...]
    slot = jnp.concatenate([slot_ref[k : k + 1, :] for k in range(pieces)], axis=1)
    match = lax.broadcasted_iota(jnp.int32, (owners, pan), 0) == owner
    match_f = jnp.where(match, 1.0, 0.0)
    stacked = jnp.concatenate(
        [match_f[:, k * LANES : (k + 1) * LANES] for k in range(pieces)], axis=0
    ).astype(BF)
    running = jnp.dot(stacked, triangle, preferred_element_type=F32)
    offset = jnp.zeros((owners, 1), F32)
    ranks = []
    for k in range(pieces):
        piece = running[k * owners : (k + 1) * owners] + offset
        picked = match_f[:, k * LANES : (k + 1) * LANES] * piece
        ranks.append(jnp.sum(picked, axis=0, keepdims=True) - 1.0)
        offset = piece[:, LANES - 1 : LANES]
    rank = jnp.concatenate(ranks, axis=1)
    rank_ref[...] = rank
    high = (slot >> 6).astype(F32)
    low = (slot & 63).astype(F32)
    weights = jnp.concatenate([match_f * high, match_f * low], axis=0).astype(BF)
    for place in range(LANES // cap):
        spread = hot(LANES, (rank + float(place * cap)).astype(BF))
        slots_ref[place] = lax.dot_general(weights, spread, NT, preferred_element_type=F32)
    copies[2].wait()
    write_messages(1, cap, owners // 2, owner, rank, rec_ref[...], slots_ref, cross_ref)


def pack_own_kernel(cap, owner_ref, rank_ref, slots_ref, rec_ref, own_ref):
    chips = slots_ref.shape[1] // 4
    write_messages(
        0, cap, chips, owner_ref[...], rank_ref[...], rec_ref[...], slots_ref, own_ref
    )


def merge_kernel(cap, own_ref, cross_ref, *out_refs):
    for j, ref in enumerate(out_refs):
        ref[0:cap] = own_ref[j, 0:cap]
        ref[cap : 2 * cap] = cross_ref[j, 0:cap]
        ref[2 * cap :] = own_ref[j, cap:] + cross_ref[j, cap:]


CHUNK = 256


def loads_at(slots, records, base, rows):
    key = slots - base.astype(F32)
    key = jnp.where((key >= 0.0) & (key < float(rows)), key, -1.0).astype(BF)
    return jnp.dot(hot(rows, key), records, preferred_element_type=F32)


def land(cap, got_refs, records_ref):
    share = LANES // cap
    order = [(ref, x) for ref in got_refs for x in range(2)]
    for k, ref in enumerate(got_refs):
        records_ref[2 * k * cap : 2 * (k + 1) * cap, :] = ref[0 : 2 * cap, :]
    rows = []
    for group in range(len(order) // share):
        row = None
        for ref, x in order[group * share : (group + 1) * share]:
            tail = ref[2 * cap :, :].astype(F32)
            part = tail[2 * x : 2 * x + 1] * 64.0 + tail[2 * x + 1 : 2 * x + 2]
            row = part if row is None else row + part
        rows.append(row)
    return jnp.concatenate(rows, axis=1)


def early_kernel(cap, count, *refs):
    got_refs, (sum_ref, records_ref) = refs[:count], refs[count:]
    slots = land(cap, got_refs, records_ref)
    records = records_ref[...]
    for k in range(sum_ref.shape[0] // CHUNK):
        at = k * CHUNK
        sum_ref[at : at + CHUNK, :] = loads_at(slots, records, jnp.int32(at), CHUNK)


def far_kernel(cap, count, *refs):
    got_refs, (sum_ref, far_ref, slots_ref, records_ref) = refs[:count], refs[count:]
    slots = land(cap, got_refs, records_ref)
    slots_ref[...] = slots
    halo = far_ref.shape[0]
    first = jnp.where(odd_core() == 1, sum_ref.shape[0] - halo, 0)
    records = records_ref[...]
    for k in range(halo // CHUNK):
        base = first + k * CHUNK
        start = sum_ref[pl.ds(pl.multiple_of(base, CHUNK), CHUNK), :]
        far_ref[k * CHUNK : (k + 1) * CHUNK, :] = (
            start + loads_at(slots, records, base, CHUNK)
        ).astype(BF)


def near_kernel(sum_ref, slots_ref, records_ref, near_ref):
    halo = near_ref.shape[0]
    first = jnp.where(odd_core() == 1, 0, sum_ref.shape[0] - halo)
    for k in range(halo // CHUNK):
        base = first + k * CHUNK
        start = sum_ref[pl.ds(pl.multiple_of(base, CHUNK), CHUNK), :]
        near_ref[k * CHUNK : (k + 1) * CHUNK, :] = (
            start + loads_at(slots_ref[...], records_ref[...], base, CHUNK)
        ).astype(BF)


def stiffen(stiff_ref, cols_ref, loads_ref, block, first_col):
    size = stiff_ref.shape[2]
    total = None
    for j in range(stiff_ref.shape[1]):
        start = pl.multiple_of((cols_ref[j, block] - first_col) * size, 32)
        part = jnp.dot(
            stiff_ref[block, j], loads_ref[pl.ds(start, size), :], preferred_element_type=F32
        )
        total = part if total is None else total + part
    return total.astype(BF)


def middle_kernel(
    sum_ref, slots_ref, records_ref, near_ref, far_ref, stiff_ref, cols_ref, loads_ref, st_ref
):
    elem_rows = loads_ref.shape[0]
    halo = near_ref.shape[0]
    blocks, _, size, _ = stiff_ref.shape
    odd = odd_core()
    last = elem_rows - halo
    near_at = pl.multiple_of(jnp.where(odd == 1, 0, last), 32)
    far_at = pl.multiple_of(jnp.where(odd == 1, last, 0), 32)
    loads_ref[pl.ds(near_at, halo), :] = near_ref[...]
    loads_ref[pl.ds(far_at, halo), :] = far_ref[...]
    for k in range((last - halo) // CHUNK):
        base = halo + k * CHUNK
        loads_ref[base : base + CHUNK, :] = (
            sum_ref[base : base + CHUNK, :]
            + loads_at(slots_ref[...], records_ref[...], jnp.int32(base), CHUNK)
        ).astype(BF)
    first_col = lax.axis_index("elem") * blocks
    for b in range(REACH, blocks - REACH):
        st_ref[(b - REACH) * size : (b - REACH + 1) * size, :] = stiffen(
            stiff_ref, cols_ref, loads_ref, b, first_col
        )


def outer_rows(side, loads_ref, got_ref, stiff_ref, cols_ref, st_ref, ext_ref):
    halo = got_ref.shape[0]
    blocks, _, size, _ = stiff_ref.shape
    end = halo + loads_ref.shape[0]
    got_at = pl.multiple_of(side * end, 32)
    ext_ref[halo:end, :] = loads_ref[...]
    ext_ref[pl.ds(got_at, halo), :] = got_ref[...]
    first_col = lax.axis_index("elem") * blocks - REACH
    for k in range(REACH):
        st_ref[k * size : (k + 1) * size, :] = stiffen(
            stiff_ref, cols_ref, ext_ref, side * (blocks - REACH) + k, first_col
        )


def near_rows_kernel(
    loads_ref, got_ref, stiff_ref, cols_ref, modes_ref, mid_ref, st_ref, modal_ref, ext_ref
):
    side = 1 - odd_core()
    outer_rows(side, loads_ref, got_ref, stiff_ref, cols_ref, st_ref, ext_ref)
    halo = got_ref.shape[0]
    last = modes_ref.shape[0] - halo
    at = pl.multiple_of(side * last, 32)
    modal_ref[...] = lax.dot_general(
        mid_ref[...], modes_ref[halo:last, :], TN, preferred_element_type=F32
    ) + lax.dot_general(
        st_ref[...], modes_ref[pl.ds(at, halo), :], TN, preferred_element_type=F32
    )


def far_rows_kernel(
    loads_ref, got_ref, stiff_ref, cols_ref, modes_ref, near_ref, modal_ref,
    edge_ref, keep_ref, send_ref, ext_ref, st_ref, total_ref,
):
    odd = odd_core()
    outer_rows(odd, loads_ref, got_ref, stiff_ref, cols_ref, st_ref, ext_ref)
    halo = got_ref.shape[0]
    last = modes_ref.shape[0] - halo
    at = pl.multiple_of(odd * last, 32)
    total_ref[...] = modal_ref[...] + lax.dot_general(
        st_ref[...], modes_ref[pl.ds(at, halo), :], TN, preferred_element_type=F32
    )
    half = total_ref.shape[0] // 2
    keep_ref[...] = total_ref[pl.ds(pl.multiple_of(odd * half, 8), half), :]
    send_ref[...] = total_ref[pl.ds(pl.multiple_of((1 - odd) * half, 8), half), :]
    edge_ref[pl.ds(pl.multiple_of(odd * halo, 32), halo), :] = st_ref[...]
    edge_ref[pl.ds(pl.multiple_of((1 - odd) * halo, 32), halo), :] = near_ref[...]


def pair_kernel(mine_ref, other_ref, keep_ref, send_ref, total_ref):
    bit = lax.rem(lax.axis_index("elem") // 2, 2)
    total_ref[...] = mine_ref[...] + other_ref[...]
    half = total_ref.shape[0] // 2
    keep_ref[...] = total_ref[pl.ds(pl.multiple_of(bit * half, 8), half), :]
    send_ref[...] = total_ref[pl.ds(pl.multiple_of((1 - bit) * half, 8), half), :].astype(BF)


def add_kernel(mine_ref, other_ref, total_ref, send_ref):
    total = mine_ref[...] + other_ref[...].astype(F32)
    total_ref[...] = total
    send_ref[...] = total.astype(BF)


def split_kernel(a_ref, high_ref, low_ref):
    a = a_ref[...].T
    high = a.astype(BF)
    high_ref[...] = high
    low_ref[...] = (a - high.astype(F32)).astype(BF)


def admit_kernel(count, mine_ref, *refs):
    others, (high_ref, low_ref, adj_ref) = refs[:count], refs[count:]
    total = mine_ref[...]
    for other in others:
        total += other[...].astype(F32)
    high = total.astype(BF)
    low = (total - high.astype(F32)).astype(BF)
    both = lax.dot_general(
        jnp.concatenate([high, low], axis=0), high_ref[...], NN, preferred_element_type=F32
    )
    rows = mine_ref.shape[0]
    adj = both[:rows] + both[rows:]
    adj += lax.dot_general(high, low_ref[...], NN, preferred_element_type=F32)
    adj_ref[...] = adj.astype(BF)


def turn_kernel(modes_ref, mid_ref, edge_ref, modes_t_ref, st_t_ref):
    elem_rows = modes_ref.shape[0]
    halo = edge_ref.shape[0] // 2
    last = elem_rows - halo
    for k in range(elem_rows // CHUNK):
        at = k * CHUNK
        modes_t_ref[:, at : at + CHUNK] = modes_ref[at : at + CHUNK, :].T
    st_t_ref[:, 0:halo] = edge_ref[0:halo, :].T
    st_t_ref[:, halo:last] = mid_ref[...].T
    st_t_ref[:, last:] = edge_ref[halo:, :].T


def back_kernel(
    own_ref, y_ref, core_ref, both_ref, modes_ref, st_ref, adj_hbm, sens_hbm,
    adj_ref, sens_ref, field_ref, sems,
):
    me = lax.axis_index("elem")
    odd = lax.rem(me, 2)
    bit = lax.rem(me // 2, 2)
    quarter = own_ref.shape[0]
    for ref, c, y in (
        (own_ref, odd, bit),
        (y_ref, odd, 1 - bit),
        (core_ref, 1 - odd, bit),
        (both_ref, 1 - odd, 1 - bit),
    ):
        at = pl.multiple_of((2 * c + y) * quarter, 16)
        field_ref[pl.ds(at, quarter), :] = ref[...]
    field = field_ref[...]
    elem_rows = modes_ref.shape[1]
    leaving = []
    for k in range(elem_rows // CHUNK):
        at = k * CHUNK
        part = jnp.dot(field, modes_ref[:, at : at + CHUNK], preferred_element_type=F32)
        row = jnp.sum(part * st_ref[:, at : at + CHUNK].astype(F32), axis=0, keepdims=True)
        for i in range(CHUNK // LANES):
            cols = slice(i * LANES, (i + 1) * LANES)
            adj_ref[at + i * LANES : at + (i + 1) * LANES, :] = part[:, cols].T.astype(BF)
            sens_ref[at // LANES + i : at // LANES + i + 1, :] = row[:, cols]
        rows = pl.ds(at, CHUNK)
        leaving.append(pltpu.make_async_copy(adj_ref.at[rows], adj_hbm.at[rows], sems.at[k]))
        leaving[-1].start()
    leaving.append(pltpu.make_async_copy(sens_ref, sens_hbm, sems.at[elem_rows // CHUNK]))
    leaving[-1].start()
    for copy in leaving:
        copy.wait()


def body(records, panel_owner, panel_slot, stiff_blocks, block_cols, modes, admittance):
    owners = lax.axis_size("elem")
    chips = owners // 2
    pan, width = records.shape
    cap = 2 * pan // owners
    share = LANES // cap
    elem_rows, mode_count = modes.shape
    blocks, nnz, size, _ = stiff_blocks.shape
    halo = REACH * size
    message = (chips, cap + TAIL, width)

    def stay(array):
        return pltpu.with_memory_space_constraint(array, pltpu.HBM)

    def swap(array, mask):
        return lax.ppermute(array, "elem", [(i, i ^ mask) for i in range(owners)])

    def swap_far(array):
        pairs = [(i, i + 1) for i in range(1, owners - 1, 2)]
        return lax.ppermute(array, "elem", pairs + [(j, i) for i, j in pairs])

    def turn(array, dz, dy):
        pairs = []
        for i in range(owners):
            z, y, core = i // 4, i // 2 % 2, i % 2
            pairs.append((i, ((z + dz) % (chips // 2) * 2 + (y + dy) % 2) * 2 + core))
        return lax.ppermute(array, "elem", pairs)

    cross, owner, rank, slots, held = call(
        functools.partial(pack_kernel, cap),
        (
            shape(message, BF),
            shape((1, pan), jnp.int32),
            shape((1, pan), F32),
            shape((share, 2 * owners, LANES), F32),
            shape((pan, width), BF),
        ),
        stay(panel_owner.reshape(1, pan)),
        stay(panel_slot.reshape(pan // LANES, LANES)),
        stay(records),
        hbm=(0, 1, 2),
        scratch=(
            pltpu.VMEM((pan // LANES, LANES), jnp.int32),
            pltpu.SemaphoreType.DMA((3,)),
        ),
        flops=owners * cap * pan * width,
    )
    got_cross = swap(cross, 1)
    own = call(
        functools.partial(pack_own_kernel, cap),
        shape(message, BF),
        owner, rank, slots, held,
        flops=owners * cap * pan * width,
    )
    packed = call(
        functools.partial(merge_kernel, cap),
        (shape((2 * cap + TAIL, width), BF),) * chips,
        own, got_cross,
    )
    offsets = list(range(1, chips))
    if share == 1:
        reach = chips // 2
        offsets.sort(key=lambda j: (-(j % 2), -min(j // 2, reach - j // 2), j))
    got = {j: turn(packed[j], j // 2, j % 2) for j in offsets}
    got[0] = packed[0]
    arrival = [0, *offsets]
    half = chips // 2
    late_rows = half * 2 * cap
    early = call(
        functools.partial(early_kernel, cap, half),
        shape((elem_rows, width), F32),
        *[got[j] for j in arrival[:half]],
        scratch=(pltpu.VMEM((late_rows, width), BF),),
        flops=2 * late_rows * elem_rows * width,
    )
    far, slot_row, landed = call(
        functools.partial(far_kernel, cap, chips - half),
        (shape((halo, width), BF), shape((1, late_rows), F32), shape((late_rows, width), BF)),
        *[got[j] for j in arrival[half:]], early,
        flops=16 * late_rows * halo * width,
    )
    got_far = swap_far(far)
    near = call(
        near_kernel,
        shape((halo, width), BF),
        early, slot_row, landed,
        flops=2 * late_rows * halo * width,
    )
    got_near = swap(near, 1)
    cols = block_cols.T
    loads, st_mid = call(
        middle_kernel,
        (shape((elem_rows, width), BF), shape((elem_rows - 2 * halo, width), BF)),
        early, slot_row, landed, near, far, stiff_blocks, cols,
        smem=(6,),
        flops=4 * late_rows * halo * width,
    )
    extended = pltpu.VMEM((elem_rows + 2 * halo, width), BF)
    st_near, modal_near = call(
        near_rows_kernel,
        (shape((halo, width), BF), shape((width, mode_count), F32)),
        loads, got_near, stiff_blocks, cols, modes, st_mid,
        smem=(3,),
        scratch=(extended,),
        flops=2 * (elem_rows - halo) * width * mode_count,
    )
    st_edge, keep, send = call(
        far_rows_kernel,
        (
            shape((2 * halo, width), BF),
            shape((width // 2, mode_count), F32),
            shape((width // 2, mode_count), F32),
        ),
        loads, got_far, stiff_blocks, cols, modes, st_near, modal_near,
        smem=(3,),
        scratch=(extended, pltpu.VMEM((halo, width), BF), pltpu.VMEM((width, mode_count), F32)),
        flops=2 * halo * width * mode_count,
    )
    quarter = width // 4
    piece = shape((quarter, mode_count), BF)
    keep, send = call(
        pair_kernel,
        (shape((quarter, mode_count), F32), piece),
        keep, swap(send, 1),
        scratch=(pltpu.VMEM((width // 2, mode_count), F32),),
    )
    total, send = call(
        add_kernel, (shape((quarter, mode_count), F32), piece), keep, swap(send, 2)
    )
    groups = chips // 2
    steps = range(groups - 1, 0, -1)
    others = [turn(send, k, 0) for k in steps]
    a_high, a_low = call(
        split_kernel,
        (shape(admittance.shape, BF), shape(admittance.shape, BF)),
        admittance,
        flops=4 * admittance.size,
    )
    mine = call(
        functools.partial(admit_kernel, len(others)),
        piece,
        total, *others, a_high, a_low,
        flops=6 * quarter * mode_count * mode_count,
    )
    across = swap(mine, 2)
    beside = swap(mine, 1)
    modes_t, st_t = call(
        turn_kernel,
        (shape((mode_count, elem_rows), BF), shape((width, elem_rows), BF)),
        modes, st_mid, st_edge,
    )
    across, modes_t, st_t = lax.optimization_barrier((across, modes_t, st_t))
    both = swap(across, 1)
    adjoint, sensitivity = call(
        back_kernel,
        (shape((elem_rows, width), BF), shape((elem_rows // LANES, LANES), F32)),
        mine, across, beside, both, modes_t, st_t,
        out=pltpu.HBM,
        scratch=(
            pltpu.VMEM((elem_rows, width), BF),
            pltpu.VMEM((elem_rows // LANES, LANES), F32),
            pltpu.VMEM((width, mode_count), BF),
            pltpu.SemaphoreType.DMA((elem_rows // CHUNK + 1,)),
        ),
        flops=2 * elem_rows * width * mode_count,
    )
    return adjoint, sensitivity.reshape(elem_rows)


def solution(mesh):
    in_specs = (
        P(("case", "elem"), None),
        P("elem", None),
        P("elem"),
        P("elem", None, None, None),
        P("elem", None),
        P("elem", None),
        P("case", None),
    )
    out_specs = (P(("case", "elem"), None), P(("case", "elem")))
    return jax.shard_map(body, mesh=mesh, in_specs=in_specs, out_specs=out_specs, check_vma=False)
```

```python
import functools

import jax
import jax.numpy as jnp
from jax import lax
from jax.experimental import pallas as pl
from jax.experimental.pallas import tpu as pltpu
from jax.sharding import PartitionSpec as P

LANES = 128
TAIL = 16
REACH = 8
BF = jnp.bfloat16
F32 = jnp.float32
NT = (((1,), (1,)), ((), ()))
NN = (((1,), (0,)), ((), ()))
TN = (((0,), (0,)), ((), ()))


def call(kernel, out_shape, *operands, smem=(), hbm=(), out=pltpu.VMEM, scratch=(), flops=0, limit=16 * 2**20):
    space = [
        pltpu.SMEM if k in smem else pltpu.HBM if k in hbm else pltpu.VMEM
        for k in range(len(operands))
    ]
    moved = sum(x.size * x.dtype.itemsize for x in operands)
    return pl.pallas_call(
        kernel,
        out_shape=out_shape,
        in_specs=[pl.BlockSpec(memory_space=s) for s in space],
        out_specs=jax.tree.map(lambda _: pl.BlockSpec(memory_space=out), out_shape),
        scratch_shapes=list(scratch),
        compiler_params=pltpu.CompilerParams(vmem_limit_bytes=limit),
        cost_estimate=pl.CostEstimate(flops=flops, bytes_accessed=moved, transcendentals=0),
    )(*operands)


def shape(dims, dtype):
    return jax.ShapeDtypeStruct(dims, dtype)


def odd_core():
    return lax.rem(lax.axis_index("elem"), 2)


def hot(rows, key):
    row = lax.broadcasted_iota(jnp.int32, (rows, key.shape[1]), 0).astype(F32).astype(BF)
    return jnp.where(row == key, jnp.ones((), BF), jnp.zeros((), BF))


def write_messages(cross, cap, chips, owner, rank, records, slots_ref, out_ref):
    me = lax.axis_index("elem")
    core = lax.rem(me + cross, 2)
    y, z = lax.rem(me // 2, 2), me // 4
    share, owners = LANES // cap, 2 * chips
    tail_row = lax.broadcasted_iota(jnp.int32, (TAIL, LANES), 0) - 2 * cross
    for j in range(chips):
        dz, dy = j // 2, j % 2
        to = (lax.rem(z + dz, chips // 2) * 2 + lax.rem(y + dy, 2)) * 2 + core
        key = jnp.where(owner == to, rank, -1.0).astype(BF)
        out_ref[j, 0:cap, :] = jnp.dot(
            hot(cap, key), records, preferred_element_type=F32
        ).astype(BF)
        place = (dy * 2 + cross) % share
        high = slots_ref[place, pl.ds(to, 1), :]
        low = slots_ref[place, pl.ds(owners + to, 1), :]
        tail = jnp.where(tail_row == 0, high, jnp.where(tail_row == 1, low, 0.0))
        out_ref[j, cap : cap + TAIL, :] = tail.astype(BF)


def pack_kernel(
    cap, owner_hbm, slot_hbm, rec_hbm, cross_ref, owner_ref, rank_ref, slots_ref, rec_ref,
    slot_ref, sems,
):
    copies = [
        pltpu.make_async_copy(source, target, sems.at[k])
        for k, (source, target) in enumerate(
            ((owner_hbm, owner_ref), (slot_hbm, slot_ref), (rec_hbm, rec_ref))
        )
    ]
    for copy in copies:
        copy.start()
    pan = rec_ref.shape[0]
    owners = slots_ref.shape[1] // 2
    pieces = pan // LANES
    before = lax.broadcasted_iota(jnp.int32, (LANES, LANES), 0)
    after = lax.broadcasted_iota(jnp.int32, (LANES, LANES), 1)
    triangle = jnp.where(before <= after, 1.0, 0.0).astype(BF)
    copies[0].wait()
    copies[1].wait()
    owner = owner_ref[...]
    slot = jnp.concatenate([slot_ref[k : k + 1, :] for k in range(pieces)], axis=1)
    match = lax.broadcasted_iota(jnp.int32, (owners, pan), 0) == owner
    match_f = jnp.where(match, 1.0, 0.0)
    stacked = jnp.concatenate(
        [match_f[:, k * LANES : (k + 1) * LANES] for k in range(pieces)], axis=0
    ).astype(BF)
    running = jnp.dot(stacked, triangle, preferred_element_type=F32)
    offset = jnp.zeros((owners, 1), F32)
    ranks = []
    for k in range(pieces):
        piece = running[k * owners : (k + 1) * owners] + offset
        picked = match_f[:, k * LANES : (k + 1) * LANES] * piece
        ranks.append(jnp.sum(picked, axis=0, keepdims=True) - 1.0)
        offset = piece[:, LANES - 1 : LANES]
    rank = jnp.concatenate(ranks, axis=1)
    rank_ref[...] = rank
    high = (slot >> 6).astype(F32)
    low = (slot & 63).astype(F32)
    weights = jnp.concatenate([match_f * high, match_f * low], axis=0).astype(BF)
    for place in range(LANES // cap):
        spread = hot(LANES, (rank + float(place * cap)).astype(BF))
        slots_ref[place] = lax.dot_general(weights, spread, NT, preferred_element_type=F32)
    copies[2].wait()
    write_messages(1, cap, owners // 2, owner, rank, rec_ref[...], slots_ref, cross_ref)


def pack_own_kernel(cap, owner_ref, rank_ref, slots_ref, rec_ref, own_ref):
    chips = slots_ref.shape[1] // 4
    write_messages(
        0, cap, chips, owner_ref[...], rank_ref[...], rec_ref[...], slots_ref, own_ref
    )


def merge_kernel(cap, own_ref, cross_ref, *out_refs):
    for j, ref in enumerate(out_refs):
        ref[0:cap] = own_ref[j, 0:cap]
        ref[cap : 2 * cap] = cross_ref[j, 0:cap]
        ref[2 * cap :] = own_ref[j, cap:] + cross_ref[j, cap:]


CHUNK = 256


def loads_at(slots, records, base, rows):
    key = slots - base.astype(F32)
    key = jnp.where((key >= 0.0) & (key < float(rows)), key, -1.0).astype(BF)
    return jnp.dot(hot(rows, key), records, preferred_element_type=F32)


def land(cap, got_refs, records_ref):
    share = LANES // cap
    order = [(ref, x) for ref in got_refs for x in range(2)]
    for k, ref in enumerate(got_refs):
        records_ref[2 * k * cap : 2 * (k + 1) * cap, :] = ref[0 : 2 * cap, :]
    rows = []
    for group in range(len(order) // share):
        row = None
        for ref, x in order[group * share : (group + 1) * share]:
            tail = ref[2 * cap :, :].astype(F32)
            part = tail[2 * x : 2 * x + 1] * 64.0 + tail[2 * x + 1 : 2 * x + 2]
            row = part if row is None else row + part
        rows.append(row)
    return jnp.concatenate(rows, axis=1)


def early_kernel(cap, count, *refs):
    got_refs, (sum_ref, records_ref) = refs[:count], refs[count:]
    slots = land(cap, got_refs, records_ref)
    records = records_ref[...]
    for k in range(sum_ref.shape[0] // CHUNK):
        at = k * CHUNK
        sum_ref[at : at + CHUNK, :] = loads_at(slots, records, jnp.int32(at), CHUNK)


def far_kernel(cap, count, *refs):
    got_refs, (sum_ref, far_ref, slots_ref, records_ref) = refs[:count], refs[count:]
    slots = land(cap, got_refs, records_ref)
    slots_ref[...] = slots
    halo = far_ref.shape[0]
    first = jnp.where(odd_core() == 1, sum_ref.shape[0] - halo, 0)
    records = records_ref[...]
    for k in range(halo // CHUNK):
        base = first + k * CHUNK
        start = sum_ref[pl.ds(pl.multiple_of(base, CHUNK), CHUNK), :]
        far_ref[k * CHUNK : (k + 1) * CHUNK, :] = (
            start + loads_at(slots, records, base, CHUNK)
        ).astype(BF)


def near_kernel(sum_ref, slots_ref, records_ref, near_ref):
    halo = near_ref.shape[0]
    first = jnp.where(odd_core() == 1, 0, sum_ref.shape[0] - halo)
    for k in range(halo // CHUNK):
        base = first + k * CHUNK
        start = sum_ref[pl.ds(pl.multiple_of(base, CHUNK), CHUNK), :]
        near_ref[k * CHUNK : (k + 1) * CHUNK, :] = (
            start + loads_at(slots_ref[...], records_ref[...], base, CHUNK)
        ).astype(BF)


def stiffen(stiff_ref, cols_ref, loads_ref, block, first_col):
    size = stiff_ref.shape[2]
    total = None
    for j in range(stiff_ref.shape[1]):
        start = pl.multiple_of((cols_ref[j, block] - first_col) * size, 32)
        part = jnp.dot(
            stiff_ref[block, j], loads_ref[pl.ds(start, size), :], preferred_element_type=F32
        )
        total = part if total is None else total + part
    return total.astype(BF)


def middle_kernel(
    sum_ref, slots_ref, records_ref, near_ref, far_ref, stiff_ref, cols_ref, loads_ref, st_ref
):
    elem_rows = loads_ref.shape[0]
    halo = near_ref.shape[0]
    blocks, _, size, _ = stiff_ref.shape
    odd = odd_core()
    last = elem_rows - halo
    near_at = pl.multiple_of(jnp.where(odd == 1, 0, last), 32)
    far_at = pl.multiple_of(jnp.where(odd == 1, last, 0), 32)
    loads_ref[pl.ds(near_at, halo), :] = near_ref[...]
    loads_ref[pl.ds(far_at, halo), :] = far_ref[...]
    for k in range((last - halo) // CHUNK):
        base = halo + k * CHUNK
        loads_ref[base : base + CHUNK, :] = (
            sum_ref[base : base + CHUNK, :]
            + loads_at(slots_ref[...], records_ref[...], jnp.int32(base), CHUNK)
        ).astype(BF)
    first_col = lax.axis_index("elem") * blocks
    for b in range(REACH, blocks - REACH):
        st_ref[(b - REACH) * size : (b - REACH + 1) * size, :] = stiffen(
            stiff_ref, cols_ref, loads_ref, b, first_col
        )


def outer_rows(side, loads_ref, got_ref, stiff_ref, cols_ref, st_ref, ext_ref, copy=None):
    halo = got_ref.shape[0]
    blocks, _, size, _ = stiff_ref.shape
    end = halo + loads_ref.shape[0]
    got_at = pl.multiple_of(side * end, 32)
    ext_ref[halo:end, :] = loads_ref[...]
    ext_ref[pl.ds(got_at, halo), :] = got_ref[...]
    if copy is not None:
        copy.wait()
    first_col = lax.axis_index("elem") * blocks - REACH
    for k in range(REACH):
        st_ref[k * size : (k + 1) * size, :] = stiffen(
            stiff_ref, cols_ref, ext_ref, side * (blocks - REACH) + k, first_col
        )


def near_rows_kernel(
    loads_ref, got_ref, stiff_ref, cols_ref, modes_ref, mid_ref, st_ref, modal_ref, ext_ref
):
    side = 1 - odd_core()
    outer_rows(side, loads_ref, got_ref, stiff_ref, cols_ref, st_ref, ext_ref)
    halo = got_ref.shape[0]
    last = modes_ref.shape[0] - halo
    at = pl.multiple_of(side * last, 32)
    modal_ref[...] = lax.dot_general(
        mid_ref[...], modes_ref[halo:last, :], TN, preferred_element_type=F32
    ) + lax.dot_general(
        st_ref[...], modes_ref[pl.ds(at, halo), :], TN, preferred_element_type=F32
    )


def far_rows_kernel(
    loads_ref, got_ref, stiff_ref, cols_vmem, modes_ref, near_ref, modal_ref,
    edge_ref, keep_ref, send_ref, ext_ref, st_ref, total_ref, cols_ref, sem,
):
    copy = pltpu.make_async_copy(cols_vmem, cols_ref, sem)
    copy.start()
    odd = odd_core()
    edge_ref[pl.ds(pl.multiple_of((1 - odd) * got_ref.shape[0], 32), got_ref.shape[0]), :] = (
        near_ref[...]
    )
    outer_rows(odd, loads_ref, got_ref, stiff_ref, cols_ref, st_ref, ext_ref, copy)
    halo = got_ref.shape[0]
    last = modes_ref.shape[0] - halo
    at = pl.multiple_of(odd * last, 32)
    total_ref[...] = modal_ref[...] + lax.dot_general(
        st_ref[...], modes_ref[pl.ds(at, halo), :], TN, preferred_element_type=F32
    )
    half = total_ref.shape[0] // 2
    keep_ref[...] = total_ref[pl.ds(pl.multiple_of(odd * half, 8), half), :]
    send_ref[...] = total_ref[pl.ds(pl.multiple_of((1 - odd) * half, 8), half), :]
    edge_ref[pl.ds(pl.multiple_of(odd * halo, 32), halo), :] = st_ref[...]


def pair_kernel(mine_ref, other_ref, keep_ref, send_ref, total_ref):
    bit = lax.rem(lax.axis_index("elem") // 2, 2)
    total_ref[...] = mine_ref[...] + other_ref[...]
    half = total_ref.shape[0] // 2
    keep_ref[...] = total_ref[pl.ds(pl.multiple_of(bit * half, 8), half), :]
    send_ref[...] = total_ref[pl.ds(pl.multiple_of((1 - bit) * half, 8), half), :].astype(BF)


def add_kernel(mine_ref, other_ref, total_ref, send_ref):
    total = mine_ref[...] + other_ref[...].astype(F32)
    total_ref[...] = total
    send_ref[...] = total.astype(BF)


def split_kernel(a_ref, high_ref, low_ref):
    a = a_ref[...].T
    high = a.astype(BF)
    high_ref[...] = high
    low_ref[...] = (a - high.astype(F32)).astype(BF)


def admit_kernel(count, mine_ref, *refs):
    others, (high_ref, low_ref, adj_ref) = refs[:count], refs[count:]
    total = mine_ref[...]
    for other in others:
        total += other[...].astype(F32)
    high = total.astype(BF)
    low = (total - high.astype(F32)).astype(BF)
    both = lax.dot_general(
        jnp.concatenate([high, low], axis=0), high_ref[...], NN, preferred_element_type=F32
    )
    rows = mine_ref.shape[0]
    adj = both[:rows] + both[rows:]
    adj += lax.dot_general(high, low_ref[...], NN, preferred_element_type=F32)
    adj_ref[...] = adj.astype(BF)


def turn_kernel(modes_ref, mid_ref, edge_ref, modes_t_ref, st_t_ref):
    elem_rows = modes_ref.shape[0]
    halo = edge_ref.shape[0] // 2
    last = elem_rows - halo
    for k in range(elem_rows // CHUNK):
        at = k * CHUNK
        modes_t_ref[:, at : at + CHUNK] = modes_ref[at : at + CHUNK, :].T
    st_t_ref[:, 0:halo] = edge_ref[0:halo, :].T
    st_t_ref[:, halo:last] = mid_ref[...].T
    st_t_ref[:, last:] = edge_ref[halo:, :].T


def back_kernel(
    own_ref, y_ref, core_ref, both_ref, modes_ref, st_ref, adj_hbm, sens_hbm,
    adj_ref, sens_ref, field_ref, sems,
):
    me = lax.axis_index("elem")
    odd = lax.rem(me, 2)
    bit = lax.rem(me // 2, 2)
    quarter = own_ref.shape[0]
    for ref, c, y in (
        (own_ref, odd, bit),
        (y_ref, odd, 1 - bit),
        (core_ref, 1 - odd, bit),
        (both_ref, 1 - odd, 1 - bit),
    ):
        at = pl.multiple_of((2 * c + y) * quarter, 16)
        field_ref[pl.ds(at, quarter), :] = ref[...]
    field = field_ref[...]
    elem_rows = modes_ref.shape[1]
    leaving = []
    for k in range(elem_rows // CHUNK):
        at = k * CHUNK
        part = jnp.dot(field, modes_ref[:, at : at + CHUNK], preferred_element_type=F32)
        row = jnp.sum(part * st_ref[:, at : at + CHUNK].astype(F32), axis=0, keepdims=True)
        for i in range(CHUNK // LANES):
            cols = slice(i * LANES, (i + 1) * LANES)
            adj_ref[at + i * LANES : at + (i + 1) * LANES, :] = part[:, cols].T.astype(BF)
            sens_ref[at // LANES + i : at // LANES + i + 1, :] = row[:, cols]
        rows = pl.ds(at, CHUNK)
        leaving.append(pltpu.make_async_copy(adj_ref.at[rows], adj_hbm.at[rows], sems.at[k]))
        leaving[-1].start()
    leaving.append(pltpu.make_async_copy(sens_ref, sens_hbm, sems.at[elem_rows // CHUNK]))
    leaving[-1].start()
    for copy in leaving:
        copy.wait()


def body(records, panel_owner, panel_slot, stiff_blocks, block_cols, modes, admittance):
    owners = lax.axis_size("elem")
    chips = owners // 2
    pan, width = records.shape
    cap = 2 * pan // owners
    share = LANES // cap
    elem_rows, mode_count = modes.shape
    blocks, nnz, size, _ = stiff_blocks.shape
    halo = REACH * size
    message = (chips, cap + TAIL, width)

    def stay(array):
        return pltpu.with_memory_space_constraint(array, pltpu.HBM)

    def swap(array, mask):
        return lax.ppermute(array, "elem", [(i, i ^ mask) for i in range(owners)])

    def swap_far(array):
        pairs = [(i, i + 1) for i in range(1, owners - 1, 2)]
        return lax.ppermute(array, "elem", pairs + [(j, i) for i, j in pairs])

    def turn(array, dz, dy):
        pairs = []
        for i in range(owners):
            z, y, core = i // 4, i // 2 % 2, i % 2
            pairs.append((i, ((z + dz) % (chips // 2) * 2 + (y + dy) % 2) * 2 + core))
        return lax.ppermute(array, "elem", pairs)

    cross, owner, rank, slots, held = call(
        functools.partial(pack_kernel, cap),
        (
            shape(message, BF),
            shape((1, pan), jnp.int32),
            shape((1, pan), F32),
            shape((share, 2 * owners, LANES), F32),
            shape((pan, width), BF),
        ),
        stay(panel_owner.reshape(1, pan)),
        stay(panel_slot.reshape(pan // LANES, LANES)),
        stay(records),
        hbm=(0, 1, 2),
        scratch=(
            pltpu.VMEM((pan // LANES, LANES), jnp.int32),
            pltpu.SemaphoreType.DMA((3,)),
        ),
        flops=owners * cap * pan * width,
    )
    got_cross = swap(cross, 1)
    own = call(
        functools.partial(pack_own_kernel, cap),
        shape(message, BF),
        owner, rank, slots, held,
        flops=owners * cap * pan * width,
    )
    packed = call(
        functools.partial(merge_kernel, cap),
        (shape((2 * cap + TAIL, width), BF),) * chips,
        own, got_cross,
    )
    offsets = list(range(1, chips))
    if share == 1:
        reach = chips // 2
        offsets.sort(key=lambda j: (-(j % 2), -min(j // 2, reach - j // 2), j))
    got = {j: turn(packed[j], j // 2, j % 2) for j in offsets}
    got[0] = packed[0]
    arrival = [0, *offsets]
    half = chips // 2
    late_rows = half * 2 * cap
    early = call(
        functools.partial(early_kernel, cap, half),
        shape((elem_rows, width), F32),
        *[got[j] for j in arrival[:half]],
        scratch=(pltpu.VMEM((late_rows, width), BF),),
        flops=2 * late_rows * elem_rows * width,
    )
    far, slot_row, landed = call(
        functools.partial(far_kernel, cap, chips - half),
        (shape((halo, width), BF), shape((1, late_rows), F32), shape((late_rows, width), BF)),
        *[got[j] for j in arrival[half:]], early,
        flops=16 * late_rows * halo * width,
    )
    got_far = swap_far(far)
    near = call(
        near_kernel,
        shape((halo, width), BF),
        early, slot_row, landed,
        flops=2 * late_rows * halo * width,
    )
    got_near = swap(near, 1)
    cols = block_cols.T
    loads, st_mid = call(
        middle_kernel,
        (shape((elem_rows, width), BF), shape((elem_rows - 2 * halo, width), BF)),
        early, slot_row, landed, near, far, stiff_blocks, cols,
        smem=(6,),
        flops=4 * late_rows * halo * width,
    )
    extended = pltpu.VMEM((elem_rows + 2 * halo, width), BF)
    st_near, modal_near = call(
        near_rows_kernel,
        (shape((halo, width), BF), shape((width, mode_count), F32)),
        loads, got_near, stiff_blocks, cols, modes, st_mid,
        smem=(3,),
        scratch=(extended,),
        flops=2 * (elem_rows - halo) * width * mode_count,
    )
    st_edge, keep, send = call(
        far_rows_kernel,
        (
            shape((2 * halo, width), BF),
            shape((width // 2, mode_count), F32),
            shape((width // 2, mode_count), F32),
        ),
        loads, got_far, stiff_blocks, cols, modes, st_near, modal_near,
        scratch=(
            extended,
            pltpu.VMEM((halo, width), BF),
            pltpu.VMEM((width, mode_count), F32),
            pltpu.SMEM(cols.shape, jnp.int32),
            pltpu.SemaphoreType.DMA(()),
        ),
        flops=2 * halo * width * mode_count,
    )
    quarter = width // 4
    piece = shape((quarter, mode_count), BF)
    keep, send = call(
        pair_kernel,
        (shape((quarter, mode_count), F32), piece),
        keep, swap(send, 1),
        scratch=(pltpu.VMEM((width // 2, mode_count), F32),),
    )
    total, send = call(
        add_kernel, (shape((quarter, mode_count), F32), piece), keep, swap(send, 2)
    )
    groups = chips // 2
    steps = range(groups - 1, 0, -1)
    others = [turn(send, k, 0) for k in steps]
    a_high, a_low = call(
        split_kernel,
        (shape(admittance.shape, BF), shape(admittance.shape, BF)),
        admittance,
        flops=4 * admittance.size,
    )
    mine = call(
        functools.partial(admit_kernel, len(others)),
        piece,
        total, *others, a_high, a_low,
        flops=6 * quarter * mode_count * mode_count,
    )
    across = swap(mine, 2)
    beside = swap(mine, 1)
    modes_t, st_t = call(
        turn_kernel,
        (shape((mode_count, elem_rows), BF), shape((width, elem_rows), BF)),
        modes, st_mid, st_edge,
    )
    across, modes_t, st_t = lax.optimization_barrier((across, modes_t, st_t))
    both = swap(across, 1)
    adjoint, sensitivity = call(
        back_kernel,
        (shape((elem_rows, width), BF), shape((elem_rows // LANES, LANES), F32)),
        mine, across, beside, both, modes_t, st_t,
        out=pltpu.HBM,
        scratch=(
            pltpu.VMEM((elem_rows, width), BF),
            pltpu.VMEM((elem_rows // LANES, LANES), F32),
            pltpu.VMEM((width, mode_count), BF),
            pltpu.SemaphoreType.DMA((elem_rows // CHUNK + 1,)),
        ),
        flops=2 * elem_rows * width * mode_count,
    )
    return adjoint, sensitivity.reshape(elem_rows)


def solution(mesh):
    in_specs = (
        P(("case", "elem"), None),
        P("elem", None),
        P("elem"),
        P("elem", None, None, None),
        P("elem", None),
        P("elem", None),
        P("case", None),
    )
    out_specs = (P(("case", "elem"), None), P(("case", "elem")))
    return jax.shard_map(body, mesh=mesh, in_specs=in_specs, out_specs=out_specs, check_vma=False)
```

```python
import functools

import jax
import jax.numpy as jnp
from jax import lax
from jax.experimental import pallas as pl
from jax.experimental.pallas import tpu as pltpu
from jax.sharding import PartitionSpec as P

LANES = 128
TAIL = 16
REACH = 8
BF = jnp.bfloat16
F32 = jnp.float32
NT = (((1,), (1,)), ((), ()))
NN = (((1,), (0,)), ((), ()))
TN = (((0,), (0,)), ((), ()))


def call(kernel, out_shape, *operands, smem=(), hbm=(), out=pltpu.VMEM, scratch=(), flops=0, limit=16 * 2**20):
    space = [
        pltpu.SMEM if k in smem else pltpu.HBM if k in hbm else pltpu.VMEM
        for k in range(len(operands))
    ]
    moved = sum(x.size * x.dtype.itemsize for x in operands)
    return pl.pallas_call(
        kernel,
        out_shape=out_shape,
        in_specs=[pl.BlockSpec(memory_space=s) for s in space],
        out_specs=jax.tree.map(lambda _: pl.BlockSpec(memory_space=out), out_shape),
        scratch_shapes=list(scratch),
        compiler_params=pltpu.CompilerParams(vmem_limit_bytes=limit),
        cost_estimate=pl.CostEstimate(flops=flops, bytes_accessed=moved, transcendentals=0),
    )(*operands)


def shape(dims, dtype):
    return jax.ShapeDtypeStruct(dims, dtype)


def odd_core():
    return lax.rem(lax.axis_index("elem"), 2)


def hot(rows, key):
    row = lax.broadcasted_iota(jnp.int32, (rows, key.shape[1]), 0).astype(F32).astype(BF)
    return jnp.where(row == key, jnp.ones((), BF), jnp.zeros((), BF))


def write_messages(cross, cap, chips, owner, rank, records, slots_ref, out_ref):
    me = lax.axis_index("elem")
    core = lax.rem(me + cross, 2)
    y, z = lax.rem(me // 2, 2), me // 4
    share, owners = LANES // cap, 2 * chips
    tail_row = lax.broadcasted_iota(jnp.int32, (TAIL, LANES), 0) - 2 * cross
    for j in range(chips):
        dz, dy = j // 2, j % 2
        to = (lax.rem(z + dz, chips // 2) * 2 + lax.rem(y + dy, 2)) * 2 + core
        key = jnp.where(owner == to, rank, -1.0).astype(BF)
        out_ref[j, 0:cap, :] = jnp.dot(
            hot(cap, key), records, preferred_element_type=F32
        ).astype(BF)
        place = (dy * 2 + cross) % share
        high = slots_ref[place, pl.ds(to, 1), :]
        low = slots_ref[place, pl.ds(owners + to, 1), :]
        tail = jnp.where(tail_row == 0, high, jnp.where(tail_row == 1, low, 0.0))
        out_ref[j, cap : cap + TAIL, :] = tail.astype(BF)


def pack_kernel(
    cap, owner_hbm, slot_hbm, rec_hbm, cross_ref, owner_ref, rank_ref, slots_ref, rec_ref,
    slot_ref, sems,
):
    copies = [
        pltpu.make_async_copy(source, target, sems.at[k])
        for k, (source, target) in enumerate(
            ((owner_hbm, owner_ref), (slot_hbm, slot_ref), (rec_hbm, rec_ref))
        )
    ]
    for copy in copies:
        copy.start()
    pan = rec_ref.shape[0]
    owners = slots_ref.shape[1] // 2
    pieces = pan // LANES
    before = lax.broadcasted_iota(jnp.int32, (LANES, LANES), 0)
    after = lax.broadcasted_iota(jnp.int32, (LANES, LANES), 1)
    triangle = jnp.where(before <= after, 1.0, 0.0).astype(BF)
    copies[0].wait()
    copies[1].wait()
    owner = owner_ref[...]
    slot = jnp.concatenate([slot_ref[k : k + 1, :] for k in range(pieces)], axis=1)
    match = lax.broadcasted_iota(jnp.int32, (owners, pan), 0) == owner
    match_f = jnp.where(match, 1.0, 0.0)
    stacked = jnp.concatenate(
        [match_f[:, k * LANES : (k + 1) * LANES] for k in range(pieces)], axis=0
    ).astype(BF)
    running = jnp.dot(stacked, triangle, preferred_element_type=F32)
    offset = jnp.zeros((owners, 1), F32)
    ranks = []
    for k in range(pieces):
        piece = running[k * owners : (k + 1) * owners] + offset
        picked = match_f[:, k * LANES : (k + 1) * LANES] * piece
        ranks.append(jnp.sum(picked, axis=0, keepdims=True) - 1.0)
        offset = piece[:, LANES - 1 : LANES]
    rank = jnp.concatenate(ranks, axis=1)
    rank_ref[...] = rank
    high = (slot >> 6).astype(F32)
    low = (slot & 63).astype(F32)
    weights = jnp.concatenate([match_f * high, match_f * low], axis=0).astype(BF)
    for place in range(LANES // cap):
        spread = hot(LANES, (rank + float(place * cap)).astype(BF))
        slots_ref[place] = lax.dot_general(weights, spread, NT, preferred_element_type=F32)
    copies[2].wait()
    write_messages(1, cap, owners // 2, owner, rank, rec_ref[...], slots_ref, cross_ref)


def pack_own_kernel(cap, owner_ref, rank_ref, slots_ref, rec_ref, own_ref):
    chips = slots_ref.shape[1] // 4
    write_messages(
        0, cap, chips, owner_ref[...], rank_ref[...], rec_ref[...], slots_ref, own_ref
    )


def merge_kernel(cap, own_ref, cross_ref, *out_refs):
    for j, ref in enumerate(out_refs):
        ref[0:cap] = own_ref[j, 0:cap]
        ref[cap : 2 * cap] = cross_ref[j, 0:cap]
        ref[2 * cap :] = own_ref[j, cap:] + cross_ref[j, cap:]


CHUNK = 256


def loads_at(slots, records, base, rows):
    key = slots - base.astype(F32)
    key = jnp.where((key >= 0.0) & (key < float(rows)), key, -1.0).astype(BF)
    return jnp.dot(hot(rows, key), records, preferred_element_type=F32)


def land(cap, got_refs, records_ref):
    share = LANES // cap
    order = [(ref, x) for ref in got_refs for x in range(2)]
    for k, ref in enumerate(got_refs):
        records_ref[2 * k * cap : 2 * (k + 1) * cap, :] = ref[0 : 2 * cap, :]
    rows = []
    for group in range(len(order) // share):
        row = None
        for ref, x in order[group * share : (group + 1) * share]:
            tail = ref[2 * cap :, :].astype(F32)
            part = tail[2 * x : 2 * x + 1] * 64.0 + tail[2 * x + 1 : 2 * x + 2]
            row = part if row is None else row + part
        rows.append(row)
    return jnp.concatenate(rows, axis=1)


def early_kernel(cap, count, *refs):
    got_refs, (sum_ref, records_ref) = refs[:count], refs[count:]
    slots = land(cap, got_refs, records_ref)
    records = records_ref[...]
    for k in range(sum_ref.shape[0] // CHUNK):
        at = k * CHUNK
        sum_ref[at : at + CHUNK, :] = loads_at(slots, records, jnp.int32(at), CHUNK)


def far_kernel(cap, count, *refs):
    got_refs, (sum_ref, far_ref, slots_ref, records_ref) = refs[:count], refs[count:]
    slots = land(cap, got_refs, records_ref)
    slots_ref[...] = slots
    halo = far_ref.shape[0]
    first = jnp.where(odd_core() == 1, sum_ref.shape[0] - halo, 0)
    records = records_ref[...]
    for k in range(halo // CHUNK):
        base = first + k * CHUNK
        start = sum_ref[pl.ds(pl.multiple_of(base, CHUNK), CHUNK), :]
        far_ref[k * CHUNK : (k + 1) * CHUNK, :] = (
            start + loads_at(slots, records, base, CHUNK)
        ).astype(BF)


def near_kernel(sum_ref, slots_ref, records_ref, near_ref):
    halo = near_ref.shape[0]
    first = jnp.where(odd_core() == 1, 0, sum_ref.shape[0] - halo)
    for k in range(halo // CHUNK):
        base = first + k * CHUNK
        start = sum_ref[pl.ds(pl.multiple_of(base, CHUNK), CHUNK), :]
        near_ref[k * CHUNK : (k + 1) * CHUNK, :] = (
            start + loads_at(slots_ref[...], records_ref[...], base, CHUNK)
        ).astype(BF)


def stiffen(stiff_ref, cols_ref, loads_ref, block, first_col):
    size = stiff_ref.shape[2]
    total = None
    for j in range(stiff_ref.shape[1]):
        start = pl.multiple_of((cols_ref[j, block] - first_col) * size, 32)
        part = jnp.dot(
            stiff_ref[block, j], loads_ref[pl.ds(start, size), :], preferred_element_type=F32
        )
        total = part if total is None else total + part
    return total.astype(BF)


def middle_kernel(
    sum_ref, slots_ref, records_ref, near_ref, far_ref, stiff_ref, cols_ref, loads_ref, st_ref
):
    elem_rows = loads_ref.shape[0]
    halo = near_ref.shape[0]
    blocks, _, size, _ = stiff_ref.shape
    odd = odd_core()
    last = elem_rows - halo
    near_at = pl.multiple_of(jnp.where(odd == 1, 0, last), 32)
    far_at = pl.multiple_of(jnp.where(odd == 1, last, 0), 32)
    loads_ref[pl.ds(near_at, halo), :] = near_ref[...]
    loads_ref[pl.ds(far_at, halo), :] = far_ref[...]
    for k in range((last - halo) // CHUNK):
        base = halo + k * CHUNK
        loads_ref[base : base + CHUNK, :] = (
            sum_ref[base : base + CHUNK, :]
            + loads_at(slots_ref[...], records_ref[...], jnp.int32(base), CHUNK)
        ).astype(BF)
    first_col = lax.axis_index("elem") * blocks
    for b in range(REACH, blocks - REACH):
        st_ref[(b - REACH) * size : (b - REACH + 1) * size, :] = stiffen(
            stiff_ref, cols_ref, loads_ref, b, first_col
        )


def outer_rows(side, loads_ref, got_ref, stiff_ref, cols_ref, st_ref, ext_ref, copy=None):
    halo = got_ref.shape[0]
    blocks, _, size, _ = stiff_ref.shape
    end = halo + loads_ref.shape[0]
    got_at = pl.multiple_of(side * end, 32)
    ext_ref[halo:end, :] = loads_ref[...]
    ext_ref[pl.ds(got_at, halo), :] = got_ref[...]
    if copy is not None:
        copy.wait()
    first_col = lax.axis_index("elem") * blocks - REACH
    for k in range(REACH):
        st_ref[k * size : (k + 1) * size, :] = stiffen(
            stiff_ref, cols_ref, ext_ref, side * (blocks - REACH) + k, first_col
        )


def near_rows_kernel(
    loads_ref, got_ref, stiff_ref, cols_ref, modes_ref, mid_ref, st_ref, modal_ref, ext_ref
):
    side = 1 - odd_core()
    outer_rows(side, loads_ref, got_ref, stiff_ref, cols_ref, st_ref, ext_ref)
    halo = got_ref.shape[0]
    last = modes_ref.shape[0] - halo
    at = pl.multiple_of(side * last, 32)
    modal_ref[...] = lax.dot_general(
        mid_ref[...], modes_ref[halo:last, :], TN, preferred_element_type=F32
    ) + lax.dot_general(
        st_ref[...], modes_ref[pl.ds(at, halo), :], TN, preferred_element_type=F32
    )


def far_rows_kernel(
    loads_ref, got_ref, stiff_ref, cols_vmem, modes_ref, near_ref, modal_ref,
    edge_ref, keep_ref, one_ref, two_ref, three_ref, ext_ref, st_ref, total_ref, cols_ref, sem,
):
    copy = pltpu.make_async_copy(cols_vmem, cols_ref, sem)
    copy.start()
    odd = odd_core()
    edge_ref[pl.ds(pl.multiple_of((1 - odd) * got_ref.shape[0], 32), got_ref.shape[0]), :] = (
        near_ref[...]
    )
    outer_rows(odd, loads_ref, got_ref, stiff_ref, cols_ref, st_ref, ext_ref, copy)
    halo = got_ref.shape[0]
    last = modes_ref.shape[0] - halo
    at = pl.multiple_of(odd * last, 32)
    total_ref[...] = modal_ref[...] + lax.dot_general(
        st_ref[...], modes_ref[pl.ds(at, halo), :], TN, preferred_element_type=F32
    )
    quarter = keep_ref.shape[0]
    part = lax.rem(lax.axis_index("elem"), 4)
    for k, ref in enumerate((keep_ref, one_ref, two_ref, three_ref)):
        to = lax.rem(part + k, 4)
        at = pl.multiple_of((lax.rem(to, 2) * 2 + to // 2) * quarter, 16)
        ref[...] = total_ref[pl.ds(at, quarter), :].astype(ref.dtype)
    edge_ref[pl.ds(pl.multiple_of(odd * halo, 32), halo), :] = st_ref[...]


def add_kernel(mine_ref, one_ref, two_ref, three_ref, total_ref, send_ref):
    total = mine_ref[...] + one_ref[...].astype(F32)
    total += two_ref[...].astype(F32) + three_ref[...].astype(F32)
    total_ref[...] = total
    send_ref[...] = total.astype(BF)


def split_kernel(a_ref, high_ref, low_ref):
    a = a_ref[...].T
    high = a.astype(BF)
    high_ref[...] = high
    low_ref[...] = (a - high.astype(F32)).astype(BF)


def admit_kernel(count, mine_ref, *refs):
    others, (high_ref, low_ref, adj_ref) = refs[:count], refs[count:]
    total = mine_ref[...]
    for other in others:
        total += other[...].astype(F32)
    high = total.astype(BF)
    low = (total - high.astype(F32)).astype(BF)
    both = lax.dot_general(
        jnp.concatenate([high, low], axis=0), high_ref[...], NN, preferred_element_type=F32
    )
    rows = mine_ref.shape[0]
    adj = both[:rows] + both[rows:]
    adj += lax.dot_general(high, low_ref[...], NN, preferred_element_type=F32)
    adj_ref[...] = adj.astype(BF)


def turn_kernel(modes_ref, mid_ref, edge_ref, modes_t_ref, st_t_ref):
    elem_rows = modes_ref.shape[0]
    halo = edge_ref.shape[0] // 2
    last = elem_rows - halo
    for k in range(elem_rows // CHUNK):
        at = k * CHUNK
        modes_t_ref[:, at : at + CHUNK] = modes_ref[at : at + CHUNK, :].T
    st_t_ref[:, 0:halo] = edge_ref[0:halo, :].T
    st_t_ref[:, halo:last] = mid_ref[...].T
    st_t_ref[:, last:] = edge_ref[halo:, :].T


def back_kernel(
    own_ref, y_ref, core_ref, both_ref, modes_ref, st_ref, adj_hbm, sens_hbm,
    adj_ref, sens_ref, field_ref, sems,
):
    me = lax.axis_index("elem")
    odd = lax.rem(me, 2)
    bit = lax.rem(me // 2, 2)
    quarter = own_ref.shape[0]
    for ref, c, y in (
        (own_ref, odd, bit),
        (y_ref, odd, 1 - bit),
        (core_ref, 1 - odd, bit),
        (both_ref, 1 - odd, 1 - bit),
    ):
        at = pl.multiple_of((2 * c + y) * quarter, 16)
        field_ref[pl.ds(at, quarter), :] = ref[...]
    field = field_ref[...]
    elem_rows = modes_ref.shape[1]
    leaving = []
    for k in range(elem_rows // CHUNK):
        at = k * CHUNK
        part = jnp.dot(field, modes_ref[:, at : at + CHUNK], preferred_element_type=F32)
        row = jnp.sum(part * st_ref[:, at : at + CHUNK].astype(F32), axis=0, keepdims=True)
        for i in range(CHUNK // LANES):
            cols = slice(i * LANES, (i + 1) * LANES)
            adj_ref[at + i * LANES : at + (i + 1) * LANES, :] = part[:, cols].T.astype(BF)
            sens_ref[at // LANES + i : at // LANES + i + 1, :] = row[:, cols]
        rows = pl.ds(at, CHUNK)
        leaving.append(pltpu.make_async_copy(adj_ref.at[rows], adj_hbm.at[rows], sems.at[k]))
        leaving[-1].start()
    leaving.append(pltpu.make_async_copy(sens_ref, sens_hbm, sems.at[elem_rows // CHUNK]))
    leaving[-1].start()
    for copy in leaving:
        copy.wait()


def body(records, panel_owner, panel_slot, stiff_blocks, block_cols, modes, admittance):
    owners = lax.axis_size("elem")
    chips = owners // 2
    pan, width = records.shape
    cap = 2 * pan // owners
    share = LANES // cap
    elem_rows, mode_count = modes.shape
    blocks, nnz, size, _ = stiff_blocks.shape
    halo = REACH * size
    message = (chips, cap + TAIL, width)

    def stay(array):
        return pltpu.with_memory_space_constraint(array, pltpu.HBM)

    def swap(array, mask):
        return lax.ppermute(array, "elem", [(i, i ^ mask) for i in range(owners)])

    def around(array, k):
        return lax.ppermute(
            array, "elem", [(i, i // 4 * 4 + (i + k) % 4) for i in range(owners)]
        )

    def swap_far(array):
        pairs = [(i, i + 1) for i in range(1, owners - 1, 2)]
        return lax.ppermute(array, "elem", pairs + [(j, i) for i, j in pairs])

    def turn(array, dz, dy):
        pairs = []
        for i in range(owners):
            z, y, core = i // 4, i // 2 % 2, i % 2
            pairs.append((i, ((z + dz) % (chips // 2) * 2 + (y + dy) % 2) * 2 + core))
        return lax.ppermute(array, "elem", pairs)

    cross, owner, rank, slots, held = call(
        functools.partial(pack_kernel, cap),
        (
            shape(message, BF),
            shape((1, pan), jnp.int32),
            shape((1, pan), F32),
            shape((share, 2 * owners, LANES), F32),
            shape((pan, width), BF),
        ),
        stay(panel_owner.reshape(1, pan)),
        stay(panel_slot.reshape(pan // LANES, LANES)),
        stay(records),
        hbm=(0, 1, 2),
        scratch=(
            pltpu.VMEM((pan // LANES, LANES), jnp.int32),
            pltpu.SemaphoreType.DMA((3,)),
        ),
        flops=owners * cap * pan * width,
    )
    got_cross = swap(cross, 1)
    own = call(
        functools.partial(pack_own_kernel, cap),
        shape(message, BF),
        owner, rank, slots, held,
        flops=owners * cap * pan * width,
    )
    packed = call(
        functools.partial(merge_kernel, cap),
        (shape((2 * cap + TAIL, width), BF),) * chips,
        own, got_cross,
    )
    offsets = list(range(1, chips))
    if share == 1:
        reach = chips // 2
        offsets.sort(key=lambda j: (-(j % 2), -min(j // 2, reach - j // 2), j))
    got = {j: turn(packed[j], j // 2, j % 2) for j in offsets}
    got[0] = packed[0]
    arrival = [0, *offsets]
    half = chips // 2
    late_rows = half * 2 * cap
    early = call(
        functools.partial(early_kernel, cap, half),
        shape((elem_rows, width), F32),
        *[got[j] for j in arrival[:half]],
        scratch=(pltpu.VMEM((late_rows, width), BF),),
        flops=2 * late_rows * elem_rows * width,
    )
    far, slot_row, landed = call(
        functools.partial(far_kernel, cap, chips - half),
        (shape((halo, width), BF), shape((1, late_rows), F32), shape((late_rows, width), BF)),
        *[got[j] for j in arrival[half:]], early,
        flops=16 * late_rows * halo * width,
    )
    got_far = swap_far(far)
    near = call(
        near_kernel,
        shape((halo, width), BF),
        early, slot_row, landed,
        flops=2 * late_rows * halo * width,
    )
    got_near = swap(near, 1)
    cols = block_cols.T
    loads, st_mid = call(
        middle_kernel,
        (shape((elem_rows, width), BF), shape((elem_rows - 2 * halo, width), BF)),
        early, slot_row, landed, near, far, stiff_blocks, cols,
        smem=(6,),
        flops=4 * late_rows * halo * width,
    )
    extended = pltpu.VMEM((elem_rows + 2 * halo, width), BF)
    st_near, modal_near = call(
        near_rows_kernel,
        (shape((halo, width), BF), shape((width, mode_count), F32)),
        loads, got_near, stiff_blocks, cols, modes, st_mid,
        smem=(3,),
        scratch=(extended,),
        flops=2 * (elem_rows - halo) * width * mode_count,
    )
    quarter = width // 4
    piece = shape((quarter, mode_count), BF)
    st_edge, keep, *sends = call(
        far_rows_kernel,
        (
            shape((2 * halo, width), BF),
            shape((quarter, mode_count), F32),
            piece,
            piece,
            piece,
        ),
        loads, got_far, stiff_blocks, cols, modes, st_near, modal_near,
        scratch=(
            extended,
            pltpu.VMEM((halo, width), BF),
            pltpu.VMEM((width, mode_count), F32),
            pltpu.SMEM(cols.shape, jnp.int32),
            pltpu.SemaphoreType.DMA(()),
        ),
        flops=2 * halo * width * mode_count,
    )
    shares = {k: around(sends[k - 1], k) for k in (1, 3, 2)}
    total, send = call(
        add_kernel,
        (shape((quarter, mode_count), F32), piece),
        keep, shares[1], shares[2], shares[3],
    )
    groups = chips // 2
    steps = range(groups - 1, 0, -1)
    others = [turn(send, k, 0) for k in steps]
    a_high, a_low = call(
        split_kernel,
        (shape(admittance.shape, BF), shape(admittance.shape, BF)),
        admittance,
        flops=4 * admittance.size,
    )
    mine = call(
        functools.partial(admit_kernel, len(others)),
        piece,
        total, *others, a_high, a_low,
        flops=6 * quarter * mode_count * mode_count,
    )
    across = swap(mine, 2)
    beside = swap(mine, 1)
    modes_t, st_t = call(
        turn_kernel,
        (shape((mode_count, elem_rows), BF), shape((width, elem_rows), BF)),
        modes, st_mid, st_edge,
    )
    across, modes_t, st_t = lax.optimization_barrier((across, modes_t, st_t))
    both = swap(across, 1)
    adjoint, sensitivity = call(
        back_kernel,
        (shape((elem_rows, width), BF), shape((elem_rows // LANES, LANES), F32)),
        mine, across, beside, both, modes_t, st_t,
        out=pltpu.HBM,
        scratch=(
            pltpu.VMEM((elem_rows, width), BF),
            pltpu.VMEM((elem_rows // LANES, LANES), F32),
            pltpu.VMEM((width, mode_count), BF),
            pltpu.SemaphoreType.DMA((elem_rows // CHUNK + 1,)),
        ),
        flops=2 * elem_rows * width * mode_count,
    )
    return adjoint, sensitivity.reshape(elem_rows)


def solution(mesh):
    in_specs = (
        P(("case", "elem"), None),
        P("elem", None),
        P("elem"),
        P("elem", None, None, None),
        P("elem", None),
        P("elem", None),
        P("case", None),
    )
    out_specs = (P(("case", "elem"), None), P(("case", "elem")))
    return jax.shard_map(body, mesh=mesh, in_specs=in_specs, out_specs=out_specs, check_vma=False)
```
